128 devices in a mesh: seq: 8 (over z, x_hi), tensor: 4 (over y), section: 4 (over x_lo, core).
Axes of the slice: x: 4 (x_hi: 2, x_lo: 2; x = x_hi * 2 + x_lo), y: 4, z: 4, core: 2. Of those that a mesh axis runs over, the one named last changes fastest.
Arguments:
- dna_bases: int32 [8, 2048, 32], P('seq', 'section'), may hold values from 0 to 3
- stem_weight: bfloat16 [128, 1536], replicated, may hold values from -1 to 1
- conv_weight: bfloat16 [3, 1536, 1536], P(None, None, 'tensor'), may hold values from -0.09375 to 0.09375
- query_weight: bfloat16 [1536, 512], P(None, 'tensor'), may hold values from -0.15625 to 0.15625
- key_weight: bfloat16 [1536, 512], P(None, 'tensor'), may hold values from -0.15625 to 0.15625
- value_weight: bfloat16 [1536, 1536], P(None, 'tensor'), may hold values from -0.15625 to 0.15625
- out_weight: bfloat16 [1536, 1536], P('tensor'), may hold values from -0.15625 to 0.15625
- cotangent: bfloat16 [8, 2048, 1536], P('seq', 'section', 'tensor'), may hold values from -6 to 6
Outputs:
- conv_grad: float32 [1536, 3, 1536], P(('seq', 'section'), None, 'tensor')
The draws below stay inside these ranges and needn't reach their ends.
All inputs are finite; a program needn't handle non-finite values.
Results may differ from the reference program's by a relative error of at most 0.013.
Values may be sent and summed in bfloat16 or wider, within the bound.
No kernel may reach another device: no remote copies, remote signals or barrier semaphores. Data moves between devices by JAX's collectives and lax.ppermute only.
A program may use at most 128 MiB of HBM per device.

```python
import math
import jax
import jax.numpy as jnp
from jax import lax

CHANNELS = 1536
HEADS = 8
KEY_SIZE = 64
VALUE_SIZE = 192
BIN_BASES = 32
DILATION = 32
TOK_DEV = 512
TOKENS = 2048
WINDOWS = 8


def place_ends(drawn, own_key, smallest, high):
    longest = drawn.shape.index(max(drawn.shape))
    spots = []
    for shift in (0, 1):
        where = [jax.random.randint(jax.random.fold_in(own_key, axis), (), 0, length) for axis, length in enumerate(drawn.shape)]
        where[longest] = (where[longest] + shift) % drawn.shape[longest]
        spots.append(tuple(where))
    return drawn.at[spots[0]].set(smallest).at[spots[1]].set(high)


def block_scale(key, shape, cuts, low, high):
    gain = 1.0
    for position, parts in cuts:
        steps = jax.random.uniform(jax.random.fold_in(jax.random.fold_in(key, 6), position), (parts,), jnp.float32, low / len(cuts), high / len(cuts))
        gain = gain * jnp.repeat(jnp.exp(steps), shape[position] // parts).reshape((-1,) + (1,) * (len(shape) - 1 - position))
    return gain


def noise(stream_key, extent, width, bound, cuts=(), kind=jnp.bfloat16):
    entries = jax.random.normal(stream_key, extent, jnp.float32) * width
    if len(cuts) > 0:
        entries = block_scale(stream_key, extent, cuts, -0.22, 0.18) * entries
    return jnp.clip(entries, min=-bound, max=bound).astype(kind)


def setup_inputs(seed: int = 0) -> dict:
    key_list = jax.random.split(jax.random.key(seed), 9)
    dna_bases = place_ends(jax.random.randint(key_list[0], (WINDOWS, TOKENS, BIN_BASES), 0, 4), jax.random.fold_in(key_list[0], 1), 0, 3).astype(jnp.int32)
    stem_weight = noise(key_list[1], (4 * BIN_BASES, CHANNELS), BIN_BASES ** -0.5, 1.0)
    conv_weight = noise(key_list[2], (3, CHANNELS, CHANNELS), (3 * CHANNELS) ** -0.5, 0.09375, ((2, 4),))
    query_weight = noise(key_list[3], (CHANNELS, HEADS * KEY_SIZE), CHANNELS ** -0.5, 0.15625, ((1, 4),))
    key_weight = noise(key_list[4], (CHANNELS, HEADS * KEY_SIZE), CHANNELS ** -0.5, 0.15625, ((1, 4),))
    value_weight = noise(key_list[5], (CHANNELS, HEADS * VALUE_SIZE), CHANNELS ** -0.5, 0.15625, ((1, 4),))
    out_weight = noise(key_list[6], (HEADS * VALUE_SIZE, CHANNELS), (HEADS * VALUE_SIZE) ** -0.5, 0.15625, ((0, 4),))
    cotangent = noise(key_list[7], (WINDOWS, TOKENS, CHANNELS), 1.0, 6.0, ((0, 8), (1, 4), (2, 4)))
    return dict(dna_bases=dna_bases, stem_weight=stem_weight, conv_weight=conv_weight, query_weight=query_weight, key_weight=key_weight, value_weight=value_weight, out_weight=out_weight, cotangent=cotangent)


EPSILON = 1e-06
SHARPNESS = 3.0

def unit_rows(raw_rows, head_size):
    shaped = raw_rows.reshape(raw_rows.shape[0], -1, head_size)
    factor = lax.rsqrt(lax.optimization_barrier(jnp.mean(shaped * shaped, axis=-1, keepdims=True)) + EPSILON)
    return ((shaped * factor).reshape(raw_rows.shape), factor)

def unit_back(grad_rows, normed, factor, head_size):
    grad_heads = grad_rows.reshape(grad_rows.shape[0], -1, head_size)
    norm_heads = normed.reshape(grad_heads.shape)
    row_mean = lax.optimization_barrier(jnp.mean(grad_heads * norm_heads, axis=-1, keepdims=True))
    return (factor * (grad_heads - norm_heads * row_mean)).reshape(grad_rows.shape)

def head_pass(query_head, key_head, value_head, grad_head, score_scale):
    block_count = TOKENS // TOK_DEV
    query_blocks = query_head.reshape(block_count, TOK_DEV, KEY_SIZE)
    grad_blocks = grad_head.reshape(block_count, TOK_DEV, VALUE_SIZE)

    def step_block(running, pieces):
        key_total, value_total = running
        query_block, grad_block = pieces
        scores = jnp.dot(query_block, key_head.T, preferred_element_type=jnp.float32) * score_scale
        exponent = jnp.exp(scores)
        totals = lax.optimization_barrier(jnp.sum(exponent, axis=1, keepdims=True))
        softmax_out = exponent / totals
        softmax_bf = softmax_out.astype(jnp.bfloat16)
        head_out = jnp.dot(softmax_bf, value_head, preferred_element_type=jnp.float32).astype(jnp.bfloat16)
        row_inner = lax.optimization_barrier(jnp.sum(grad_block.astype(jnp.float32) * head_out.astype(jnp.float32), axis=1, keepdims=True))
        prob_grad = jnp.dot(grad_block, value_head.T, preferred_element_type=jnp.float32)
        score_grad = (softmax_out * (prob_grad - row_inner) * score_scale).astype(jnp.bfloat16)
        query_grad = jnp.dot(score_grad, key_head, preferred_element_type=jnp.float32)
        key_total = key_total + jnp.dot(score_grad.T, query_block, preferred_element_type=jnp.float32)
        value_total = value_total + jnp.dot(softmax_bf.T, grad_block, preferred_element_type=jnp.float32)
        return ((key_total, value_total), query_grad)
    start_state = (jnp.zeros((TOKENS, KEY_SIZE), jnp.float32), jnp.zeros((TOKENS, VALUE_SIZE), jnp.float32))
    (key_total, value_total), query_grads = lax.scan(step_block, start_state, (query_blocks, grad_blocks))
    return (query_grads.reshape(TOKENS, KEY_SIZE), key_total, value_total)

def window_terms(bases_window, stem_weight, conv_weight, query_weight, key_weight, value_weight, out_weight, cotangent_window):
    letters = jnp.arange(4, dtype=jnp.int32)
    onehot = (bases_window[:, :, None] == letters[None, None, :]).reshape(TOKENS, 4 * BIN_BASES).astype(jnp.bfloat16)
    stem_out = jnp.dot(onehot, stem_weight, preferred_element_type=jnp.float32)
    activated = jax.nn.gelu(stem_out, approximate=True).astype(jnp.bfloat16)
    margin = jnp.zeros((DILATION, CHANNELS), jnp.bfloat16)
    padded = jnp.concatenate([margin, activated, margin], axis=0)
    windows = [padded[offset * DILATION:offset * DILATION + TOKENS] for offset in range(3)]
    conv_out = jnp.zeros((TOKENS, CHANNELS), jnp.float32)
    for offset in range(3):
        conv_out = conv_out + jnp.dot(windows[offset], conv_weight[offset], preferred_element_type=jnp.float32)
    hidden = (stem_out + conv_out).astype(jnp.bfloat16)
    query_raw = jnp.dot(hidden, query_weight, preferred_element_type=jnp.float32)
    key_raw = jnp.dot(hidden, key_weight, preferred_element_type=jnp.float32)
    values = jnp.dot(hidden, value_weight, preferred_element_type=jnp.float32).astype(jnp.bfloat16)
    query_unit, query_factor = unit_rows(query_raw, KEY_SIZE)
    key_unit, key_factor = unit_rows(key_raw, KEY_SIZE)
    query_bf = query_unit.astype(jnp.bfloat16)
    key_bf = key_unit.astype(jnp.bfloat16)
    out_grad = jnp.dot(cotangent_window, out_weight.T, preferred_element_type=jnp.float32).astype(jnp.bfloat16)
    score_scale = SHARPNESS / math.sqrt(KEY_SIZE)
    query_parts, key_parts, value_parts = ([], [], [])
    for head_index in range(HEADS):
        key_cols = slice(head_index * KEY_SIZE, (head_index + 1) * KEY_SIZE)
        value_cols = slice(head_index * VALUE_SIZE, (head_index + 1) * VALUE_SIZE)
        query_grad, key_grad, value_grad = head_pass(query_bf[:, key_cols], key_bf[:, key_cols], values[:, value_cols], out_grad[:, value_cols], score_scale)
        query_parts.append(query_grad)
        key_parts.append(key_grad)
        value_parts.append(value_grad)
    query_back = unit_back(jnp.concatenate(query_parts, axis=1), query_unit, query_factor, KEY_SIZE).astype(jnp.bfloat16)
    key_back = unit_back(jnp.concatenate(key_parts, axis=1), key_unit, key_factor, KEY_SIZE).astype(jnp.bfloat16)
    value_back = jnp.concatenate(value_parts, axis=1).astype(jnp.bfloat16)
    hidden_grad = cotangent_window.astype(jnp.float32)
    hidden_grad = hidden_grad + jnp.dot(query_back, query_weight.T, preferred_element_type=jnp.float32)
    hidden_grad = hidden_grad + jnp.dot(key_back, key_weight.T, preferred_element_type=jnp.float32)
    hidden_grad = hidden_grad + jnp.dot(value_back, value_weight.T, preferred_element_type=jnp.float32)
    hidden_grad = hidden_grad.astype(jnp.bfloat16)
    tap_terms = [jnp.dot(windows[offset].T, hidden_grad, preferred_element_type=jnp.float32) for offset in range(3)]
    return jnp.stack(tap_terms, axis=1)

def reference(dna_bases, stem_weight, conv_weight, query_weight, key_weight, value_weight, out_weight, cotangent):
    total = jnp.zeros((CHANNELS, 3, CHANNELS), jnp.float32)
    for window_index in range(WINDOWS):
        total = total + window_terms(dna_bases[window_index], stem_weight, conv_weight, query_weight, key_weight, value_weight, out_weight, cotangent[window_index])
    return total * (1.0 / math.sqrt(WINDOWS * TOKENS))
```

```python
import functools
import math

import jax
import jax.numpy as jnp
from jax import lax
from jax.experimental import pallas as pl
from jax.experimental.pallas import tpu as pltpu
from jax.sharding import PartitionSpec as P

KEY = 64
VAL = 192
HALO = 32
EPSILON = 1e-06
SCALE = 3.0 / math.sqrt(KEY)
LOG2E = math.log2(math.e)

f32 = jnp.float32
bf16 = jnp.bfloat16
MIB = 1 << 20


def nn(left, right):
    return jnp.dot(left, right, preferred_element_type=f32)


def nt(left, right):
    return lax.dot_general(left, right, (((1,), (1,)), ((), ())), preferred_element_type=f32)


def call(kernel, outs, *args, scratch=(), flops=0, vmem=32):
    size = sum(math.prod(a.shape) * a.dtype.itemsize for a in args)
    return pl.pallas_call(
        kernel,
        out_shape=[jax.ShapeDtypeStruct(shape, kind) for shape, kind in outs],
        in_specs=[pl.BlockSpec(memory_space=pltpu.VMEM)] * len(args),
        out_specs=[pl.BlockSpec(memory_space=pltpu.VMEM)] * len(outs),
        scratch_shapes=list(scratch),
        compiler_params=pltpu.CompilerParams(vmem_limit_bytes=vmem * MIB),
        cost_estimate=pl.CostEstimate(flops=int(flops), bytes_accessed=int(size), transcendentals=0),
    )(*args)


def own_chip():
    section = lax.axis_index("section")
    return section >> 1, section & 1


def block_at(index, width):
    return pl.ds(pl.multiple_of(index * width, width), width)


def one_hot(marks):
    spread = (
        lax.broadcasted_iota(jnp.int32, (32, 128), 1) >> 2
        == lax.broadcasted_iota(jnp.int32, (32, 128), 0)
    )
    spread = jnp.where(spread, 1.0, 0.0).astype(bf16)
    wide = nn(marks.astype(f32).astype(bf16), spread)
    letter = ((lax.broadcasted_iota(jnp.int32, wide.shape, 1) & 3) + 1).astype(f32)
    return jnp.where(wide == letter, 1.0, 0.0).astype(bf16)


def gelu(x):
    return jax.nn.gelu(x, approximate=True)


def stem_kernel(marks_ref, weight_ref, act_ref):
    hot = one_hot(marks_ref[...])
    for j in range(0, weight_ref.shape[1], 256):
        act_ref[:, j : j + 256] = gelu(nn(hot, weight_ref[:, j : j + 256])).astype(bf16)


def conv_kernel(marks_ref, low_ref, high_ref, stem_ref, act_ref, weight_ref, hidden_ref, ext_ref):
    rows = act_ref.shape[0]
    width = weight_ref.shape[2]
    edge = jnp.concatenate([low_ref[...], high_ref[...]], axis=0)
    hot = one_hot(edge)
    edge_act = gelu(nn(hot, stem_ref[...])).astype(bf16)
    ext_ref[0:HALO] = edge_act[:HALO]
    ext_ref[HALO : HALO + rows] = act_ref[...]
    ext_ref[HALO + rows :] = edge_act[HALO:]
    own = stem_ref[:, block_at(lax.axis_index("tensor"), width)]
    total = nn(one_hot(marks_ref[...]), own)
    for k in range(3):
        total = total + nn(ext_ref[k * HALO : k * HALO + rows], weight_ref[k])
    hidden_ref[...] = total.astype(bf16)


def turn_kernel(q_ref, k_ref, v_ref, out_ref):
    out_ref[0:128] = q_ref[...].T
    out_ref[128:256] = k_ref[...].T
    out_ref[256:640] = v_ref[...].T


def taps_kernel(ext_ref, mine_ref, other_ref, turned):
    rows = turned.shape[1]
    _, core = own_chip()
    for k in range(3):
        turned[...] = ext_ref[k * HALO : k * HALO + rows].T
        for x in range(4):
            for z in range(4):
                to = ((x * 4 + z) * 3 + k) * 48
                base = z * 384 + x * 96
                mine_ref[to : to + 48] = turned[pl.ds(pl.multiple_of(base + core * 48, 16), 48)]
                other_ref[to : to + 48] = turned[
                    pl.ds(pl.multiple_of(base + (1 - core) * 48, 16), 48)
                ]


def project_kernel(h0, h1, h2, h3, w_ref, mine_ref, other_ref, unit_ref, factor_ref, values):
    y = lax.axis_index("tensor")
    chip, _ = own_chip()
    total = nt(w_ref[:, block_at(y, 384)], h0[...])
    for d, ref in ((1, h1), (2, h2), (3, h3)):
        total = total + nt(w_ref[:, block_at(y ^ d, 384)], ref[...])
    for g in range(4):
        raw = total[g * KEY : (g + 1) * KEY]
        factor = lax.rsqrt(jnp.mean(raw * raw, axis=0, keepdims=True) + EPSILON)
        unit_ref[g * KEY : (g + 1) * KEY] = raw * factor
        factor_ref[g : g + 1] = factor
    values[...] = total[256:].astype(bf16)
    for ref, head in ((mine_ref, chip), (other_ref, 1 - chip)):
        ref[0:64] = unit_ref[block_at(head, KEY)].astype(bf16)
        ref[64:128] = unit_ref[pl.ds(pl.multiple_of(128 + head * KEY, KEY), KEY)].astype(bf16)
        ref[128:320] = values[block_at(head, VAL)]


def grad_kernel(c0, c1, c2, c3, w_ref, mine_ref, other_ref):
    y = lax.axis_index("tensor")
    chip, _ = own_chip()
    for ref, head in ((mine_ref, chip), (other_ref, 1 - chip)):
        total = nt(w_ref[block_at(head, VAL), block_at(y, 384)], c0[...])
        for d, c in ((1, c1), (2, c2), (3, c3)):
            total = total + nt(w_ref[block_at(head, VAL), block_at(y ^ d, 384)], c[...])
        ref[...] = total.astype(bf16)


def attend_kernel(
    own, par, sib_own, sib_par, g_own, g_par,
    q_own_ref, q_par_ref, kv_mine_ref, kv_sib_ref,
    kv_t, kv_n, exps, score_grads, grads, queries,
):
    sections = (own, par, sib_own, sib_par)
    n = own.shape[1]
    for i, ref in enumerate(sections):
        kv = ref[64:320]
        kv_t[:, i * n : (i + 1) * n] = kv
        kv_n[i * n : (i + 1) * n] = kv.T
    width = 256
    zeros_q = jnp.zeros((VAL, width), bf16)
    zeros_g = jnp.zeros((KEY, width), bf16)
    for b in range(2 * n // width):
        src, g_src, dst = ((own, g_own, q_own_ref), (par, g_par, q_par_ref))[b * width // n]
        cols = slice((b * width) % n, (b * width) % n + width)
        lanes = slice(b * width, (b + 1) * width)
        query = src[0:64, cols]
        queries[:, lanes] = query
        right = jnp.concatenate([query, zeros_q], axis=0)
        total = jnp.zeros((1, width), f32)
        for i in range(4):
            e = jnp.exp2(nn(kv_n[i * n : (i + 1) * n], right) * (SCALE * LOG2E))
            total = total + jnp.sum(e, axis=0, keepdims=True)
            exps[i * n : (i + 1) * n, lanes] = e.astype(bf16)
        out = nn(kv_t[64:256], exps[:, lanes])
        inverse = 1.0 / total
        grad = (g_src[:, cols].astype(f32) * inverse).astype(bf16)
        grads[:, lanes] = grad
        inner = jnp.sum(grad.astype(f32) * out, axis=0, keepdims=True) * inverse
        right = jnp.concatenate([zeros_g, grad], axis=0)
        for i in range(4):
            prob = nn(kv_n[i * n : (i + 1) * n], right)
            e = exps[i * n : (i + 1) * n, lanes].astype(f32)
            score_grads[i * n : (i + 1) * n, lanes] = (e * (prob - inner)).astype(bf16)
        dst[:, cols] = (nn(kv_t[0:64], score_grads[:, lanes]) * SCALE).astype(bf16)
    for i, ref, at in ((2, kv_sib_ref, 0), (3, kv_sib_ref, n), (0, kv_mine_ref, 0), (1, kv_mine_ref, n)):
        key_grad = nt(queries[...], score_grads[i * n : (i + 1) * n]) * SCALE
        ref[0:64, at : at + n] = key_grad.astype(ref.dtype)
        value_grad = nt(grads[...], exps[i * n : (i + 1) * n])
        ref[64:256, at : at + n] = value_grad.astype(ref.dtype)


def join_kernel(q_own, q_par, kv_mine, kv_got, own_ref, par_ref):
    n = q_own.shape[1]
    par_ref[0:64] = q_par[...]
    par_ref[64:320] = (kv_mine[:, n:] + kv_got[:, n:].astype(f32)).astype(bf16)
    own_ref[0:64] = q_own[...]
    own_ref[64:320] = (kv_mine[:, :n] + kv_got[:, :n].astype(f32)).astype(bf16)


def back_kernel(own, other, unit_ref, factor_ref, wq, wk, wv, back, to1, to2, to3):
    y = lax.axis_index("tensor")
    chip, _ = own_chip()
    for ref, head in ((own, chip), (other, 1 - chip)):
        for kind in range(2):
            at = pl.ds(pl.multiple_of(kind * 128 + head * KEY, KEY), KEY)
            unit = unit_ref[at]
            factor = factor_ref[pl.ds(kind * 2 + head, 1)]
            g = ref[kind * 64 : kind * 64 + 64].astype(f32)
            mean = jnp.mean(g * unit, axis=0, keepdims=True)
            back[at] = (factor * (g - unit * mean)).astype(bf16)
        back[pl.ds(pl.multiple_of(256 + head * VAL, 64), VAL)] = ref[128:320]
    for d, ref in ((2, to2), (1, to1), (3, to3)):
        ref[...] = back_rows(back, wq, wk, wv, y ^ d).astype(bf16)


def back_rows(back, wq, wk, wv, index):
    at = block_at(index, 384)
    qk = jnp.concatenate([wq[at], wk[at]], axis=1)
    return nn(qk, back[0:256]) + nn(wv[at], back[256:640])


def back_own_kernel(back, wq, wk, wv, cot, out_ref):
    y = lax.axis_index("tensor")
    out_ref[...] = back_rows(back, wq, wk, wv, y) + cot[...].astype(f32).T


def hidden_grad_kernel(own, r1, r2, r3, out_ref):
    out_ref[...] = (
        own[...] + r1[...].astype(f32) + r2[...].astype(f32) + r3[...].astype(f32)
    ).astype(bf16)


def ring_place():
    x = (lax.axis_index("seq") & 1) * 2 + (lax.axis_index("section") >> 1)
    z = lax.axis_index("seq") >> 1
    return x, z


def tap_kernel(d, t_mine, t_sib, g_mine, g_sib, out_ref):
    x, _ = ring_place()
    at = block_at(x ^ d, 576)
    out_ref[...] = (nt(t_mine[at], g_mine[...]) + nt(t_sib[at], g_sib[...])).astype(out_ref.dtype)


def sum_x_kernel(own, r1, r2, r3, own_ref, to1, to2, to3):
    _, z = ring_place()
    for d, ref in ((2, to2), (1, to1), (3, to3), (0, own_ref)):
        at = block_at(z ^ d, 144)
        ref[...] = (
            own[at] + r1[at].astype(f32) + r2[at].astype(f32) + r3[at].astype(f32)
        ).astype(ref.dtype)


def sum_z_kernel(norm, own, r1, r2, r3, out_ref):
    out_ref[...] = (
        own[...] + r1[...].astype(f32) + r2[...].astype(f32) + r3[...].astype(f32)
    ) * norm


def body(bases, stem_w, conv_w, wq, wk, wv, out_w, cot):
    marks = bases[0] + 1
    cot = cot[0]
    rows = marks.shape[0]
    flat = ("seq", "section")

    low = lax.ppermute(marks[rows - HALO :], "section", [(i, i + 1) for i in range(3)])
    high = lax.ppermute(marks[:HALO], "section", [(i + 1, i) for i in range(3)])

    def over_y(value, d):
        return lax.ppermute(value, "tensor", [(i, i ^ d) for i in range(4)])

    def over_core(value):
        return lax.ppermute(value, "section", [(i, i ^ 1) for i in range(4)])

    def over_chip(value):
        return lax.ppermute(value, "section", [(i, i ^ 2) for i in range(4)])

    def over_x(value, d):
        return lax.ppermute(value, flat, [(i, i ^ (2 * d)) for i in range(32)])

    def over_z(value, d):
        return lax.ppermute(value, flat, [(i, i ^ (8 * d)) for i in range(32)])

    cots = [cot] + [over_y(cot, d) for d in (1, 2, 3)]

    (act,) = call(stem_kernel, [((rows, 1536), bf16)], marks, stem_w, flops=4e8)
    hidden, ext = call(
        conv_kernel,
        [((rows, 384), bf16), ((rows + 2 * HALO, 1536), bf16)],
        marks, low, high, stem_w, act, conv_w,
        flops=2e9,
    )
    hiddens = [hidden] + [over_y(hidden, d) for d in (1, 2, 3)]

    (w_t,) = call(turn_kernel, [((640, 1536), bf16)], wq, wk, wv, flops=1e9)
    taps_mine, taps_other = call(
        taps_kernel, [((2304, rows), bf16)] * 2, ext,
        scratch=[pltpu.VMEM((1536, rows), bf16)], flops=3e9,
    )
    taps_sib = over_core(taps_other)

    g_own, g_other = call(grad_kernel, [((VAL, rows), bf16)] * 2, *cots, out_w, flops=1e9)
    g_par = over_chip(g_other)

    own, other, unit, factor = call(
        project_kernel,
        [((320, rows), bf16)] * 2 + [((256, rows), f32), ((4, rows), f32)],
        *hiddens, w_t,
        scratch=[pltpu.VMEM((384, rows), bf16)], flops=1.5e9,
    )
    par = over_chip(other)
    sib_own = over_core(own)
    sib_par = over_core(par)
    q_own, q_par, kv_mine, kv_sib = call(
        attend_kernel,
        [((KEY, rows), bf16)] * 2 + [((256, 2 * rows), f32), ((256, 2 * rows), bf16)],
        own, par, sib_own, sib_par, g_own, g_par,
        scratch=[
            pltpu.VMEM((256, 4 * rows), bf16),
            pltpu.VMEM((4 * rows, 256), bf16),
            pltpu.VMEM((4 * rows, 2 * rows), bf16),
            pltpu.VMEM((4 * rows, 2 * rows), bf16),
            pltpu.VMEM((VAL, 2 * rows), bf16),
            pltpu.VMEM((KEY, 2 * rows), bf16),
        ],
        flops=8e9, vmem=48,
    )
    kv_got = over_core(kv_sib)
    back_own, back_par = call(join_kernel, [((320, rows), bf16)] * 2, q_own, q_par, kv_mine, kv_got)
    back_other = over_chip(back_par)
    back, to1, to2, to3 = call(
        back_kernel,
        [((640, rows), bf16)] + [((384, rows), bf16)] * 3,
        back_own, back_other, unit, factor, wq, wk, wv, flops=1e9,
    )
    got = [over_y(to2, 2), over_y(to1, 1), over_y(to3, 3)]
    (grad_own,) = call(back_own_kernel, [((384, rows), f32)], back, wq, wk, wv, cot, flops=1e9)
    (hg,) = call(hidden_grad_kernel, [((384, rows), bf16)], grad_own, *got)
    hg_sib = over_core(hg)

    parts = []
    for d in (2, 1, 3, 0):
        (part,) = call(
            functools.partial(tap_kernel, d),
            [((576, 384), bf16 if d else f32)],
            taps_mine, taps_sib, hg, hg_sib, flops=6e8,
        )
        parts.append(over_x(part, d) if d else part)
    own_z, z1, z2, z3 = call(
        sum_x_kernel,
        [((144, 384), f32)] + [((144, 384), bf16)] * 3,
        parts[3], parts[0], parts[1], parts[2],
    )
    got = [over_z(z2, 2), over_z(z1, 1), over_z(z3, 3)]
    norm = 1.0 / math.sqrt(rows * 32)
    (total,) = call(functools.partial(sum_z_kernel, norm), [((144, 384), f32)], own_z, *got)
    return total.reshape(3, 48, 384).transpose(1, 0, 2)


def solution(mesh):
    in_specs = (
        P("seq", "section", None),
        P(),
        P(None, None, "tensor"),
        P(None, "tensor"),
        P(None, "tensor"),
        P(None, "tensor"),
        P("tensor", None),
        P("seq", "section", "tensor"),
    )
    out_specs = P(("seq", "section"), None, "tensor")
    return jax.shard_map(body, mesh=mesh, in_specs=in_specs, out_specs=out_specs, check_vma=False)
```

```python
import functools
import math

import jax
import jax.numpy as jnp
from jax import lax
from jax.experimental import pallas as pl
from jax.experimental.pallas import tpu as pltpu
from jax.sharding import PartitionSpec as P

KEY = 64
VAL = 192
HALO = 32
EPSILON = 1e-06
SCALE = 3.0 / math.sqrt(KEY)
LOG2E = math.log2(math.e)

f32 = jnp.float32
bf16 = jnp.bfloat16
MIB = 1 << 20


def nn(left, right):
    return jnp.dot(left, right, preferred_element_type=f32)


def nt(left, right):
    return lax.dot_general(left, right, (((1,), (1,)), ((), ())), preferred_element_type=f32)


def call(kernel, outs, *args, scratch=(), flops=0, vmem=32):
    size = sum(math.prod(a.shape) * a.dtype.itemsize for a in args)
    return pl.pallas_call(
        kernel,
        out_shape=[jax.ShapeDtypeStruct(shape, kind) for shape, kind in outs],
        in_specs=[pl.BlockSpec(memory_space=pltpu.VMEM)] * len(args),
        out_specs=[pl.BlockSpec(memory_space=pltpu.VMEM)] * len(outs),
        scratch_shapes=list(scratch),
        compiler_params=pltpu.CompilerParams(vmem_limit_bytes=vmem * MIB),
        cost_estimate=pl.CostEstimate(flops=int(flops), bytes_accessed=int(size), transcendentals=0),
    )(*args)


def own_chip():
    section = lax.axis_index("section")
    return section >> 1, section & 1


def block_at(index, width):
    return pl.ds(pl.multiple_of(index * width, width), width)


def one_hot(marks):
    spread = (
        lax.broadcasted_iota(jnp.int32, (32, 128), 1) >> 2
        == lax.broadcasted_iota(jnp.int32, (32, 128), 0)
    )
    spread = jnp.where(spread, 1.0, 0.0).astype(bf16)
    wide = nn(marks.astype(f32).astype(bf16), spread)
    letter = ((lax.broadcasted_iota(jnp.int32, wide.shape, 1) & 3) + 1).astype(f32)
    return jnp.where(wide == letter, 1.0, 0.0).astype(bf16)


def gelu(x):
    return jax.nn.gelu(x, approximate=True)


def stem_kernel(marks_ref, weight_ref, act_ref):
    hot = one_hot(marks_ref[...])
    for j in range(0, weight_ref.shape[1], 256):
        act_ref[:, j : j + 256] = gelu(nn(hot, weight_ref[:, j : j + 256])).astype(bf16)


def conv_kernel(marks_ref, low_ref, high_ref, stem_ref, act_ref, weight_ref, lo_ref, hi_ref, ext_ref):
    rows = act_ref.shape[0]
    width = weight_ref.shape[2]
    edge = jnp.concatenate([low_ref[...], high_ref[...]], axis=0)
    hot = one_hot(edge)
    edge_act = gelu(nn(hot, stem_ref[...])).astype(bf16)
    ext_ref[0:HALO] = edge_act[:HALO]
    ext_ref[HALO : HALO + rows] = act_ref[...]
    ext_ref[HALO + rows :] = edge_act[HALO:]
    own = stem_ref[:, block_at(lax.axis_index("tensor"), width)]
    total = nn(one_hot(marks_ref[...]), own)
    for k in range(3):
        total = total + nn(ext_ref[k * HALO : k * HALO + rows], weight_ref[k])
    lo_ref[...] = total[: rows // 2].astype(bf16)
    hi_ref[...] = total[rows // 2 :].astype(bf16)


def turn_kernel(q_ref, k_ref, v_ref, out_ref):
    out_ref[0:128] = q_ref[...].T
    out_ref[128:256] = k_ref[...].T
    out_ref[256:640] = v_ref[...].T


def taps_kernel(ext_ref, mine_ref, other_ref, turned):
    rows = turned.shape[1]
    _, core = own_chip()
    for k in range(3):
        turned[...] = ext_ref[k * HALO : k * HALO + rows].T
        for x in range(4):
            for z in range(4):
                to = ((x * 4 + z) * 3 + k) * 48
                base = z * 384 + x * 96
                mine_ref[to : to + 48] = turned[pl.ds(pl.multiple_of(base + core * 48, 16), 48)]
                other_ref[to : to + 48] = turned[
                    pl.ds(pl.multiple_of(base + (1 - core) * 48, 16), 48)
                ]


def gathered(blocks):
    lo, hi, lo1, hi1, lo3, hi3, lo2, hi2 = blocks
    return ((0, lo), (1, lo1), (3, lo3), (2, lo2)), ((0, hi), (1, hi1), (3, hi3), (2, hi2))


def project_kernel(*refs):
    w_ref, mine_ref, other_ref, unit_ref, factor_ref, values = refs[8:]
    y = lax.axis_index("tensor")
    chip, _ = own_chip()
    for half, blocks in enumerate(gathered(refs[:8])):
        half_rows = blocks[0][1].shape[0]
        at = slice(half * half_rows, (half + 1) * half_rows)
        total = 0.0
        for d, ref in blocks:
            total = total + nt(w_ref[:, block_at(y ^ d, 384)], ref[...])
        for g in range(4):
            raw = total[g * KEY : (g + 1) * KEY]
            factor = lax.rsqrt(jnp.mean(raw * raw, axis=0, keepdims=True) + EPSILON)
            unit_ref[g * KEY : (g + 1) * KEY, at] = raw * factor
            factor_ref[g : g + 1, at] = factor
        values[:, at] = total[256:].astype(bf16)
    for ref, head in ((mine_ref, chip), (other_ref, 1 - chip)):
        ref[0:64] = unit_ref[block_at(head, KEY)].astype(bf16)
        ref[64:128] = unit_ref[pl.ds(pl.multiple_of(128 + head * KEY, KEY), KEY)].astype(bf16)
        ref[128:320] = values[block_at(head, VAL)]


def grad_kernel(*refs):
    w_ref, mine_ref, other_ref = refs[8:]
    y = lax.axis_index("tensor")
    chip, _ = own_chip()
    for half, blocks in enumerate(gathered(refs[:8])):
        half_rows = blocks[0][1].shape[0]
        at = slice(half * half_rows, (half + 1) * half_rows)
        for ref, head in ((mine_ref, chip), (other_ref, 1 - chip)):
            total = 0.0
            for d, block in blocks:
                total = total + nt(w_ref[block_at(head, VAL), block_at(y ^ d, 384)], block[...])
            ref[:, at] = total.astype(bf16)


def attend_kernel(
    own, par, sib_own, sib_par, g_own, g_par,
    q_own_ref, q_par_ref, kv_mine_ref, kv_sib_ref,
    kv_t, kv_n, exps, score_grads, grads, queries,
):
    sections = (own, par, sib_own, sib_par)
    n = own.shape[1]
    for i, ref in enumerate(sections):
        kv = ref[64:320]
        kv_t[:, i * n : (i + 1) * n] = kv
        kv_n[i * n : (i + 1) * n] = kv.T
    width = 256
    zeros_q = jnp.zeros((VAL, width), bf16)
    zeros_g = jnp.zeros((KEY, width), bf16)
    for b in range(2 * n // width):
        src, g_src, dst = ((own, g_own, q_own_ref), (par, g_par, q_par_ref))[b * width // n]
        cols = slice((b * width) % n, (b * width) % n + width)
        lanes = slice(b * width, (b + 1) * width)
        query = src[0:64, cols]
        queries[:, lanes] = query
        right = jnp.concatenate([query, zeros_q], axis=0)
        total = jnp.zeros((1, width), f32)
        for i in range(4):
            e = jnp.exp2(nn(kv_n[i * n : (i + 1) * n], right) * (SCALE * LOG2E))
            total = total + jnp.sum(e, axis=0, keepdims=True)
            exps[i * n : (i + 1) * n, lanes] = e.astype(bf16)
        out = nn(kv_t[64:256], exps[:, lanes])
        inverse = 1.0 / total
        grad = (g_src[:, cols].astype(f32) * inverse).astype(bf16)
        grads[:, lanes] = grad
        inner = jnp.sum(grad.astype(f32) * out, axis=0, keepdims=True) * inverse
        right = jnp.concatenate([zeros_g, grad], axis=0)
        for i in range(4):
            prob = nn(kv_n[i * n : (i + 1) * n], right)
            e = exps[i * n : (i + 1) * n, lanes].astype(f32)
            score_grads[i * n : (i + 1) * n, lanes] = (e * (prob - inner)).astype(bf16)
        dst[:, cols] = (nn(kv_t[0:64], score_grads[:, lanes]) * SCALE).astype(bf16)
    for i, ref, at in ((2, kv_sib_ref, 0), (3, kv_sib_ref, n), (0, kv_mine_ref, 0), (1, kv_mine_ref, n)):
        key_grad = nt(queries[...], score_grads[i * n : (i + 1) * n]) * SCALE
        ref[0:64, at : at + n] = key_grad.astype(ref.dtype)
        value_grad = nt(grads[...], exps[i * n : (i + 1) * n])
        ref[64:256, at : at + n] = value_grad.astype(ref.dtype)


def join_kernel(q_own, q_par, kv_mine, kv_got, own_ref, par_ref):
    n = q_own.shape[1]
    par_ref[0:64] = q_par[...]
    par_ref[64:320] = (kv_mine[:, n:] + kv_got[:, n:].astype(f32)).astype(bf16)
    own_ref[0:64] = q_own[...]
    own_ref[64:320] = (kv_mine[:, :n] + kv_got[:, :n].astype(f32)).astype(bf16)


def back_kernel(own, other, unit_ref, factor_ref, wq, wk, wv, back, to_a, to_b):
    y = lax.axis_index("tensor")
    chip, _ = own_chip()
    for ref, head in ((own, chip), (other, 1 - chip)):
        for kind in range(2):
            at = pl.ds(pl.multiple_of(kind * 128 + head * KEY, KEY), KEY)
            unit = unit_ref[at]
            factor = factor_ref[pl.ds(kind * 2 + head, 1)]
            g = ref[kind * 64 : kind * 64 + 64].astype(f32)
            mean = jnp.mean(g * unit, axis=0, keepdims=True)
            back[at] = (factor * (g - unit * mean)).astype(bf16)
        back[pl.ds(pl.multiple_of(256 + head * VAL, 64), VAL)] = ref[128:320]
    for half, ref in enumerate((to_a, to_b)):
        ref[...] = back_rows(back, wq, wk, wv, (y ^ 2) * 2 + half, 192).astype(bf16)


def back_rows(back, wq, wk, wv, index, width):
    at = block_at(index, width)
    qk = jnp.concatenate([wq[at], wk[at]], axis=1)
    return nn(qk, back[0:256]) + nn(wv[at], back[256:640])


def back_near_kernel(back, wq, wk, wv, near1_a, near1_b, near3_a, near3_b):
    y = lax.axis_index("tensor")
    for d, half, ref in ((1, 0, near1_a), (3, 1, near3_b), (3, 0, near3_a), (1, 1, near1_b)):
        ref[...] = back_rows(back, wq, wk, wv, (y ^ d) * 2 + half, 192).astype(ref.dtype)


def back_own_kernel(back, wq, wk, wv, cot_lo, cot_hi, out_ref):
    y = lax.axis_index("tensor")
    half = cot_lo.shape[0]
    total = back_rows(back, wq, wk, wv, y, 384)
    out_ref[:, :half] = total[:, :half] + cot_lo[...].astype(f32).T
    out_ref[:, half:] = total[:, half:] + cot_hi[...].astype(f32).T


def add_kernel(near3_a, got_a, near1_b, got_b, out_a, out_b):
    out_a[...] = (near3_a[...] + got_a[...].astype(f32)).astype(bf16)
    out_b[...] = (near1_b[...] + got_b[...].astype(f32)).astype(bf16)


def hidden_grad_kernel(own, got1_a, got3_b, got3_a, got1_b, out_ref):
    half = got1_a.shape[0]
    for at, left, right in ((slice(0, half), got1_a, got3_a), (slice(half, 2 * half), got1_b, got3_b)):
        out_ref[at] = (own[at] + left[...].astype(f32) + right[...].astype(f32)).astype(bf16)


def ring_place():
    x = (lax.axis_index("seq") & 1) * 2 + (lax.axis_index("section") >> 1)
    z = lax.axis_index("seq") >> 1
    return x, z


def tap_kernel(pieces, t_mine, t_sib, g_mine, g_sib, *outs):
    x, _ = ring_place()
    for (d, start, size), out_ref in zip(pieces, outs):
        at = pl.ds(pl.multiple_of((x ^ d) * 576 + start, 288), size)
        out_ref[...] = (nt(t_mine[at], g_mine[...]) + nt(t_sib[at], g_sib[...])).astype(out_ref.dtype)


def sum_x_kernel(own, got1_a, got3_b, got3_a, got1_b, own_ref, to1, to2, to3, total):
    _, z = ring_place()
    half = got1_a.shape[0]
    for at, left, right in ((slice(0, half), got1_a, got3_a), (slice(half, 2 * half), got1_b, got3_b)):
        total[at] = own[at] + left[...].astype(f32) + right[...].astype(f32)
    for d, ref in ((2, to2), (1, to1), (3, to3), (0, own_ref)):
        ref[...] = total[block_at(z ^ d, 144)].astype(ref.dtype)


def sum_z_kernel(norm, own, r1, r2, r3, out_ref):
    out_ref[...] = (
        own[...] + r1[...].astype(f32) + r2[...].astype(f32) + r3[...].astype(f32)
    ) * norm


def body(bases, stem_w, conv_w, wq, wk, wv, out_w, cot):
    marks = bases[0] + 1
    cot = cot[0]
    rows = marks.shape[0]
    flat = ("seq", "section")

    low = lax.ppermute(marks[rows - HALO :], "section", [(i, i + 1) for i in range(3)])
    high = lax.ppermute(marks[:HALO], "section", [(i + 1, i) for i in range(3)])

    def over_y(value, d):
        return lax.ppermute(value, "tensor", [(i, i ^ d) for i in range(4)])

    def over_core(value):
        return lax.ppermute(value, "section", [(i, i ^ 1) for i in range(4)])

    def over_chip(value):
        return lax.ppermute(value, "section", [(i, i ^ 2) for i in range(4)])

    def over_x(value, d):
        return lax.ppermute(value, flat, [(i, i ^ (2 * d)) for i in range(32)])

    def over_z(value, d):
        return lax.ppermute(value, flat, [(i, i ^ (8 * d)) for i in range(32)])

    def ring_gather(lo, hi, over):
        lo1, hi3 = over(lo, 1), over(hi, 3)
        hi1, lo3 = over(hi, 1), over(lo, 3)
        hi2, lo2 = over(hi3, 1), over(lo1, 3)
        return [lo, hi, lo1, hi1, lo3, hi3, lo2, hi2]

    cots = ring_gather(cot[: rows // 2], cot[rows // 2 :], over_y)

    (act,) = call(stem_kernel, [((rows, 1536), bf16)], marks, stem_w, flops=4e8)
    low, high, act, cots[2], cots[5] = lax.optimization_barrier((low, high, act, cots[2], cots[5]))
    hidden_lo, hidden_hi, ext = call(
        conv_kernel,
        [((rows // 2, 384), bf16)] * 2 + [((rows + 2 * HALO, 1536), bf16)],
        marks, low, high, stem_w, act, conv_w,
        flops=2e9,
    )
    hidden_lo, hidden_hi, cots = lax.optimization_barrier((hidden_lo, hidden_hi, cots))
    hiddens = ring_gather(hidden_lo, hidden_hi, over_y)

    (w_t,) = call(turn_kernel, [((640, 1536), bf16)], wq, wk, wv, flops=1e9)
    taps_mine, taps_other = call(
        taps_kernel, [((2304, rows), bf16)] * 2, ext,
        scratch=[pltpu.VMEM((1536, rows), bf16)], flops=3e9,
    )

    g_own, g_other = call(grad_kernel, [((VAL, rows), bf16)] * 2, *cots, out_w, flops=1e9)
    g_par = over_chip(g_other)
    hiddens, g_par, g_own, taps_mine, taps_other, w_t = lax.optimization_barrier(
        (hiddens, g_par, g_own, taps_mine, taps_other, w_t)
    )

    own, other, unit, factor = call(
        project_kernel,
        [((320, rows), bf16)] * 2 + [((256, rows), f32), ((4, rows), f32)],
        *hiddens, w_t,
        scratch=[pltpu.VMEM((384, rows), bf16)], flops=1.5e9,
    )
    par = over_chip(other)
    sib_own = over_core(own)
    sib_par = over_core(par)
    taps_sib = over_core(taps_other)
    q_own, q_par, kv_mine, kv_sib = call(
        attend_kernel,
        [((KEY, rows), bf16)] * 2 + [((256, 2 * rows), f32), ((256, 2 * rows), bf16)],
        own, par, sib_own, sib_par, g_own, g_par,
        scratch=[
            pltpu.VMEM((256, 4 * rows), bf16),
            pltpu.VMEM((4 * rows, 256), bf16),
            pltpu.VMEM((4 * rows, 2 * rows), bf16),
            pltpu.VMEM((4 * rows, 2 * rows), bf16),
            pltpu.VMEM((VAL, 2 * rows), bf16),
            pltpu.VMEM((KEY, 2 * rows), bf16),
        ],
        flops=8e9, vmem=48,
    )
    kv_got = over_core(kv_sib)
    back_own, back_par = call(join_kernel, [((320, rows), bf16)] * 2, q_own, q_par, kv_mine, kv_got)
    back_other = over_chip(back_par)
    back, far_a, far_b = call(
        back_kernel,
        [((640, rows), bf16)] + [((192, rows), bf16)] * 2,
        back_own, back_other, unit, factor, wq, wk, wv, flops=5e8,
    )
    got_a, got_b = over_y(far_a, 1), over_y(far_b, 3)
    near1_a, near1_b, near3_a, near3_b = call(
        back_near_kernel,
        [((192, rows), kind) for kind in (bf16, f32, f32, bf16)],
        back, wq, wk, wv, flops=8e8,
    )
    got1_a, got3_b = over_y(near1_a, 1), over_y(near3_b, 3)
    (grad_own,) = call(back_own_kernel, [((384, rows), f32)], back, wq, wk, wv, cots[0], cots[1], flops=5e8)
    sum_a, sum_b = call(add_kernel, [((192, rows), bf16)] * 2, near3_a, got_a, near1_b, got_b)
    got3_a, got1_b = over_y(sum_a, 3), over_y(sum_b, 1)
    (hg,) = call(hidden_grad_kernel, [((384, rows), bf16)], grad_own, got1_a, got3_b, got3_a, got1_b)
    hg_sib = over_core(hg)

    def taps(*pieces):
        return call(
            functools.partial(tap_kernel, [p[:3] for p in pieces]),
            [((p[2], 384), p[3]) for p in pieces],
            taps_mine, taps_sib, hg, hg_sib, flops=6e8,
        )

    far_a, far_b = taps((2, 0, 288, bf16), (2, 288, 288, bf16))
    got_a, got_b = over_x(far_a, 1), over_x(far_b, 3)
    near1_a, near3_b = taps((1, 0, 288, bf16), (3, 288, 288, bf16))
    got1_a, got3_b = over_x(near1_a, 1), over_x(near3_b, 3)
    near3_a, near1_b = taps((3, 0, 288, f32), (1, 288, 288, f32))
    (part,) = taps((0, 0, 576, f32))
    sum_a, sum_b = call(add_kernel, [((288, 384), bf16)] * 2, near3_a, got_a, near1_b, got_b)
    got3_a, got1_b = over_x(sum_a, 3), over_x(sum_b, 1)
    own_z, z1, z2, z3 = call(
        sum_x_kernel,
        [((144, 384), f32)] + [((144, 384), bf16)] * 3,
        part, got1_a, got3_b, got3_a, got1_b,
        scratch=[pltpu.VMEM((576, 384), f32)],
    )
    got = [over_z(z2, 2), over_z(z1, 1), over_z(z3, 3)]
    norm = 1.0 / math.sqrt(rows * 32)
    (total,) = call(functools.partial(sum_z_kernel, norm), [((144, 384), f32)], own_z, *got)
    return total.reshape(3, 48, 384).transpose(1, 0, 2)


def solution(mesh):
    in_specs = (
        P("seq", "section", None),
        P(),
        P(None, None, "tensor"),
        P(None, "tensor"),
        P(None, "tensor"),
        P(None, "tensor"),
        P("tensor", None),
        P("seq", "section", "tensor"),
    )
    out_specs = P(("seq", "section"), None, "tensor")
    return jax.shard_map(body, mesh=mesh, in_specs=in_specs, out_specs=out_specs, check_vma=False)
```

```python
import functools
import math

import jax
import jax.numpy as jnp
from jax import lax
from jax.experimental import pallas as pl
from jax.experimental.pallas import tpu as pltpu
from jax.sharding import PartitionSpec as P

KEY = 64
VAL = 192
HALO = 32
EPSILON = 1e-06
SCALE = 3.0 / math.sqrt(KEY)
LOG2E = math.log2(math.e)

f32 = jnp.float32
bf16 = jnp.bfloat16
MIB = 1 << 20


def nn(left, right):
    return jnp.dot(left, right, preferred_element_type=f32)


def nt(left, right):
    return lax.dot_general(left, right, (((1,), (1,)), ((), ())), preferred_element_type=f32)


def call(kernel, outs, *args, scratch=(), flops=0, vmem=32, hbm=()):
    size = sum(math.prod(a.shape) * a.dtype.itemsize for a in args)
    return pl.pallas_call(
        kernel,
        out_shape=[jax.ShapeDtypeStruct(shape, kind) for shape, kind in outs],
        in_specs=[
            pl.BlockSpec(memory_space=pl.ANY if i in hbm else pltpu.VMEM) for i in range(len(args))
        ],
        out_specs=[pl.BlockSpec(memory_space=pltpu.VMEM)] * len(outs),
        scratch_shapes=list(scratch),
        compiler_params=pltpu.CompilerParams(vmem_limit_bytes=vmem * MIB),
        cost_estimate=pl.CostEstimate(flops=int(flops), bytes_accessed=int(size), transcendentals=0),
    )(*args)


def own_chip():
    section = lax.axis_index("section")
    return section >> 1, section & 1


def block_at(index, width):
    return pl.ds(pl.multiple_of(index * width, width), width)


def one_hot(marks):
    shape = (128, 32)
    spread = lax.broadcasted_iota(jnp.int32, shape, 0) >> 2 == lax.broadcasted_iota(jnp.int32, shape, 1)
    spread = jnp.where(spread, 1.0, 0.0).astype(bf16)
    wide = nn(spread, marks.astype(f32).astype(bf16))
    letter = (lax.broadcasted_iota(jnp.int32, wide.shape, 0) & 3).astype(f32)
    return jnp.where(wide == letter, 1.0, 0.0).T.astype(bf16)


def gelu(x):
    return jax.nn.gelu(x, approximate=True)


def stem_kernel(marks_ref, stem_ref, weight_hbm, act_ref, weight_ref, arrived):
    copy = pltpu.make_async_copy(weight_hbm, weight_ref, arrived)
    copy.start()
    hot = one_hot(marks_ref[...])
    for j in range(0, stem_ref.shape[1], 256):
        act_ref[:, j : j + 256] = gelu(nn(hot, stem_ref[:, j : j + 256])).astype(bf16)
    copy.wait()


def conv_kernel(marks_ref, low_ref, high_ref, stem_ref, act_ref, weight_ref, hidden_ref, ext_ref):
    rows = act_ref.shape[0]
    section = lax.axis_index("section")
    edge = one_hot(jnp.concatenate([low_ref[:, rows - HALO :], high_ref[:, :HALO]], axis=1))
    edge_act = gelu(nn(edge, stem_ref[...])).astype(bf16)
    ext_ref[0:HALO] = jnp.where(section > 0, edge_act[:HALO], 0)
    ext_ref[HALO : HALO + rows] = act_ref[...]
    ext_ref[HALO + rows :] = jnp.where(section < 3, edge_act[HALO:], 0)
    total = nn(one_hot(marks_ref[...]), stem_ref[:, block_at(lax.axis_index("tensor"), 384)])
    for k in range(3):
        total = total + nn(ext_ref[k * HALO : k * HALO + rows], weight_ref[k])
    hidden_ref[...] = total.astype(bf16)


def turn_kernel(q_ref, k_ref, v_ref, out_ref):
    out_ref[0:128] = q_ref[...].T
    out_ref[128:256] = k_ref[...].T
    out_ref[256:640] = v_ref[...].T


def taps_kernel(ext_ref, mine_ref, other_ref, turned):
    rows = turned.shape[1]
    _, core = own_chip()
    for k in range(3):
        turned[...] = ext_ref[k * HALO : k * HALO + rows].T
        for x in range(4):
            for z in range(4):
                to = ((x * 4 + z) * 3 + k) * 48
                base = z * 384 + x * 96
                mine_ref[to : to + 48] = turned[pl.ds(pl.multiple_of(base + core * 48, 16), 48)]
                other_ref[to : to + 48] = turned[
                    pl.ds(pl.multiple_of(base + (1 - core) * 48, 16), 48)
                ]


def distances():
    core = lax.axis_index("section") & 1
    return 1 + 2 * core, 3 - 2 * core


def gathered(blocks):
    own, first, second, far = blocks
    one, two = distances()
    return (0, own), (one, first), (two, second), (2, far)


def project_kernel(h0, h1, h2, h3, w_ref, mine_ref, other_ref, unit_ref, factor_ref, values):
    y = lax.axis_index("tensor")
    chip, _ = own_chip()
    total = 0.0
    for d, ref in gathered((h0, h1, h2, h3)):
        total = total + nt(w_ref[:, block_at(y ^ d, 384)], ref[...])
    for g in range(4):
        raw = total[g * KEY : (g + 1) * KEY]
        factor = lax.rsqrt(jnp.mean(raw * raw, axis=0, keepdims=True) + EPSILON)
        unit_ref[g * KEY : (g + 1) * KEY] = raw * factor
        factor_ref[g : g + 1] = factor
    values[...] = total[256:].astype(bf16)
    for ref, head in ((mine_ref, chip), (other_ref, 1 - chip)):
        ref[0:64] = unit_ref[block_at(head, KEY)].astype(bf16)
        ref[64:128] = unit_ref[pl.ds(pl.multiple_of(128 + head * KEY, KEY), KEY)].astype(bf16)
        ref[128:320] = values[block_at(head, VAL)]


def grad_kernel(c0, c1, c2, c3, w_ref, mine_ref, other_ref):
    y = lax.axis_index("tensor")
    chip, _ = own_chip()
    for ref, head in ((mine_ref, chip), (other_ref, 1 - chip)):
        total = 0.0
        for d, block in gathered((c0, c1, c2, c3)):
            total = total + nt(w_ref[block_at(head, VAL), block_at(y ^ d, 384)], block[...])
        ref[...] = total.astype(bf16)


def attend_kernel(
    own, par, sib_own, sib_par, g_own, g_par,
    q_own_ref, q_par_ref, kv_mine_ref, kv_sib_ref,
    kv_t, kv_n, exps, score_grads, grads, queries,
):
    sections = (own, par, sib_own, sib_par)
    n = own.shape[1]
    for i, ref in enumerate(sections):
        kv = ref[64:320]
        kv_t[:, i * n : (i + 1) * n] = kv
        kv_n[i * n : (i + 1) * n] = kv.T
    width = 256
    zeros_q = jnp.zeros((VAL, width), bf16)
    zeros_g = jnp.zeros((KEY, width), bf16)
    for b in range(2 * n // width):
        src, g_src, dst = ((own, g_own, q_own_ref), (par, g_par, q_par_ref))[b * width // n]
        cols = slice((b * width) % n, (b * width) % n + width)
        lanes = slice(b * width, (b + 1) * width)
        query = src[0:64, cols]
        queries[:, lanes] = query
        right = jnp.concatenate([query, zeros_q], axis=0)
        total = jnp.zeros((1, width), f32)
        for i in range(4):
            e = jnp.exp2(nn(kv_n[i * n : (i + 1) * n], right) * (SCALE * LOG2E))
            total = total + jnp.sum(e, axis=0, keepdims=True)
            exps[i * n : (i + 1) * n, lanes] = e.astype(bf16)
        out = nn(kv_t[64:256], exps[:, lanes])
        inverse = 1.0 / total
        grad = (g_src[:, cols].astype(f32) * inverse).astype(bf16)
        grads[:, lanes] = grad
        inner = jnp.sum(grad.astype(f32) * out, axis=0, keepdims=True) * inverse
        right = jnp.concatenate([zeros_g, grad], axis=0)
        for i in range(4):
            prob = nn(kv_n[i * n : (i + 1) * n], right)
            e = exps[i * n : (i + 1) * n, lanes].astype(f32)
            score_grads[i * n : (i + 1) * n, lanes] = (e * (prob - inner)).astype(bf16)
        dst[:, cols] = (nn(kv_t[0:64], score_grads[:, lanes]) * SCALE).astype(bf16)
    for i, ref, at in ((2, kv_sib_ref, 0), (3, kv_sib_ref, n), (0, kv_mine_ref, 0), (1, kv_mine_ref, n)):
        key_grad = nt(queries[...], score_grads[i * n : (i + 1) * n]) * SCALE
        ref[0:64, at : at + n] = key_grad.astype(ref.dtype)
        value_grad = nt(grads[...], exps[i * n : (i + 1) * n])
        ref[64:256, at : at + n] = value_grad.astype(ref.dtype)


def join_kernel(q_own, q_par, kv_mine, kv_got, own_ref, par_ref):
    n = q_own.shape[1]
    par_ref[0:64] = q_par[...]
    par_ref[64:320] = (kv_mine[:, n:] + kv_got[:, n:].astype(f32)).astype(bf16)
    own_ref[0:64] = q_own[...]
    own_ref[64:320] = (kv_mine[:, :n] + kv_got[:, :n].astype(f32)).astype(bf16)


def back_kernel(own, other, unit_ref, factor_ref, wq, wk, wv, back, far_ref):
    y = lax.axis_index("tensor")
    chip, _ = own_chip()
    for ref, head in ((own, chip), (other, 1 - chip)):
        for kind in range(2):
            at = pl.ds(pl.multiple_of(kind * 128 + head * KEY, KEY), KEY)
            unit = unit_ref[at]
            factor = factor_ref[pl.ds(kind * 2 + head, 1)]
            g = ref[kind * 64 : kind * 64 + 64].astype(f32)
            mean = jnp.mean(g * unit, axis=0, keepdims=True)
            back[at] = (factor * (g - unit * mean)).astype(bf16)
        back[pl.ds(pl.multiple_of(256 + head * VAL, 64), VAL)] = ref[128:320]
    far_ref[...] = back_rows(back, wq, wk, wv, y ^ 2).astype(bf16)


def back_rows(back, wq, wk, wv, index):
    at = block_at(index, 384)
    qk = jnp.concatenate([wq[at], wk[at]], axis=1)
    return nn(qk, back[0:256]) + nn(wv[at], back[256:640])


def back_near_kernel(back, wq, wk, wv, alone_ref, joined_ref):
    y = lax.axis_index("tensor")
    one, two = distances()
    alone_ref[...] = back_rows(back, wq, wk, wv, y ^ one).astype(bf16)
    joined_ref[...] = back_rows(back, wq, wk, wv, y ^ two)


def back_own_kernel(back, wq, wk, wv, cot, out_ref):
    y = lax.axis_index("tensor")
    out_ref[...] = back_rows(back, wq, wk, wv, y) + cot[...].astype(f32).T


def add_kernel(joined, got, out_ref):
    out_ref[...] = (joined[...] + got[...].astype(f32)).astype(bf16)


def hidden_grad_kernel(own, alone, joined, out_ref):
    out_ref[...] = (own[...] + alone[...].astype(f32) + joined[...].astype(f32)).astype(bf16)


def ring_place():
    x = (lax.axis_index("seq") & 1) * 2 + (lax.axis_index("section") >> 1)
    z = lax.axis_index("seq") >> 1
    return x, z


def tap_kernel(which, t_mine, t_sib, g_mine, g_sib, out_ref):
    x, _ = ring_place()
    d = (0, *distances(), 2)[which]
    at = block_at(x ^ d, 576)
    out_ref[...] = (nt(t_mine[at], g_mine[...]) + nt(t_sib[at], g_sib[...])).astype(out_ref.dtype)


def sum_x_kernel(own, alone, joined, own_ref, to1, to2, to3):
    _, z = ring_place()
    for d, ref in ((2, to2), (1, to1), (3, to3), (0, own_ref)):
        at = block_at(z ^ d, 144)
        ref[...] = (own[at] + alone[at].astype(f32) + joined[at].astype(f32)).astype(ref.dtype)


def sum_z_kernel(norm, own, r1, r2, r3, out_ref):
    out_ref[...] = (
        own[...] + r1[...].astype(f32) + r2[...].astype(f32) + r3[...].astype(f32)
    ) * norm


def body(bases, stem_w, conv_w, wq, wk, wv, out_w, cot):
    marks = bases[0].T
    cot = cot[0]
    rows = marks.shape[1]
    flat = ("seq", "section")

    low = lax.ppermute(marks, "section", [(i, (i + 1) % 4) for i in range(4)])
    high = lax.ppermute(marks, "section", [((i + 1) % 4, i) for i in range(4)])

    def y_way(value, way):
        pairs = []
        for t in range(4):
            for i in range(4):
                pairs.append((t * 4 + i, (t ^ (1, 3)[(i + way) % 2]) * 4 + i))
        return lax.ppermute(value, ("tensor", "section"), pairs)

    def x_way(value, way):
        return lax.ppermute(value, flat, [(i, i ^ (2 * (1, 3)[(i + way) % 2])) for i in range(32)])

    def over_core(value):
        return lax.ppermute(value, "section", [(i, i ^ 1) for i in range(4)])

    def over_chip(value):
        return lax.ppermute(value, "section", [(i, i ^ 2) for i in range(4)])

    def over_z(value, d):
        return lax.ppermute(value, flat, [(i, i ^ (8 * d)) for i in range(32)])

    second = y_way(cot, 1)
    act, conv_here = call(
        stem_kernel, [((rows, 1536), bf16), (conv_w.shape, bf16)], marks, stem_w, conv_w,
        scratch=[pltpu.SemaphoreType.DMA(())], flops=4e8, vmem=16, hbm=(2,),
    )
    first = y_way(cot, 0)
    hidden, ext = call(
        conv_kernel,
        [((rows, 384), bf16), ((rows + 2 * HALO, 1536), bf16)],
        marks, low, high, stem_w, act, conv_here,
        flops=2e9,
    )
    far = y_way(second, 0)
    cots = (cot, first, second, far)

    second = y_way(hidden, 1)
    taps_mine, taps_other = call(
        taps_kernel, [((2304, rows), bf16)] * 2, ext,
        scratch=[pltpu.VMEM((1536, rows), bf16)], flops=3e9,
    )
    (w_t,) = call(turn_kernel, [((640, 1536), bf16)], wq, wk, wv, flops=1e9)
    first = y_way(lax.optimization_barrier((hidden, taps_mine, w_t))[0], 0)
    second, cots = lax.optimization_barrier((second, cots))
    far = y_way(second, 0)
    g_own, g_other = call(grad_kernel, [((VAL, rows), bf16)] * 2, *cots, out_w, flops=1e9)
    g_par = over_chip(g_other)
    first, second, far, g_par, g_own = lax.optimization_barrier((first, second, far, g_par, g_own))

    own, other, unit, factor = call(
        project_kernel,
        [((320, rows), bf16)] * 2 + [((256, rows), f32), ((4, rows), f32)],
        hidden, first, second, far, w_t,
        scratch=[pltpu.VMEM((384, rows), bf16)], flops=1.5e9,
    )
    par = over_chip(other)
    sib_own = over_core(own)
    sib_par = over_core(par)
    taps_sib = over_core(taps_other)
    q_own, q_par, kv_mine, kv_sib = call(
        attend_kernel,
        [((KEY, rows), bf16)] * 2 + [((256, 2 * rows), f32), ((256, 2 * rows), bf16)],
        own, par, sib_own, sib_par, g_own, g_par,
        scratch=[
            pltpu.VMEM((256, 4 * rows), bf16),
            pltpu.VMEM((4 * rows, 256), bf16),
            pltpu.VMEM((4 * rows, 2 * rows), bf16),
            pltpu.VMEM((4 * rows, 2 * rows), bf16),
            pltpu.VMEM((VAL, 2 * rows), bf16),
            pltpu.VMEM((KEY, 2 * rows), bf16),
        ],
        flops=8e9, vmem=48,
    )
    kv_got = over_core(kv_sib)
    back_own, back_par = call(join_kernel, [((320, rows), bf16)] * 2, q_own, q_par, kv_mine, kv_got)
    back_other = over_chip(back_par)
    back, far = call(
        back_kernel,
        [((640, rows), bf16), ((384, rows), bf16)],
        back_own, back_other, unit, factor, wq, wk, wv, flops=5e8,
    )
    got = y_way(far, 0)
    alone, joined = call(
        back_near_kernel, [((384, rows), bf16), ((384, rows), f32)], back, wq, wk, wv, flops=8e8
    )
    alone = y_way(alone, 0)
    (grad_own,) = call(back_own_kernel, [((384, rows), f32)], back, wq, wk, wv, cot, flops=5e8)
    (joined,) = call(add_kernel, [((384, rows), bf16)], joined, got)
    joined = y_way(joined, 1)
    (hg,) = call(hidden_grad_kernel, [((384, rows), bf16)], grad_own, alone, joined)
    hg_sib = over_core(hg)

    def product(which, kind):
        return call(
            functools.partial(tap_kernel, which),
            [((576, 384), kind)],
            taps_mine, taps_sib, hg, hg_sib, flops=6e8,
        )[0]

    got = x_way(product(3, bf16), 0)
    alone = x_way(product(1, bf16), 0)
    joined = product(2, f32)
    part = product(0, f32)
    (joined,) = call(add_kernel, [((576, 384), bf16)], joined, got)
    joined = x_way(joined, 1)
    own_z, z1, z2, z3 = call(
        sum_x_kernel, [((144, 384), f32)] + [((144, 384), bf16)] * 3, part, alone, joined
    )
    got = [over_z(z2, 2), over_z(z1, 1), over_z(z3, 3)]
    norm = 1.0 / math.sqrt(rows * 32)
    (total,) = call(functools.partial(sum_z_kernel, norm), [((144, 384), f32)], own_z, *got)
    return total.reshape(3, 48, 384).transpose(1, 0, 2)


def solution(mesh):
    in_specs = (
        P("seq", "section", None),
        P(),
        P(None, None, "tensor"),
        P(None, "tensor"),
        P(None, "tensor"),
        P(None, "tensor"),
        P("tensor", None),
        P("seq", "section", "tensor"),
    )
    out_specs = P(("seq", "section"), None, "tensor")
    return jax.shard_map(body, mesh=mesh, in_specs=in_specs, out_specs=out_specs, check_vma=False)
```

```python
import functools
import math

import jax
import jax.numpy as jnp
from jax import lax
from jax.experimental import pallas as pl
from jax.experimental.pallas import tpu as pltpu
from jax.sharding import PartitionSpec as P

KEY = 64
VAL = 192
HALO = 32
EPSILON = 1e-06
SCALE = 3.0 / math.sqrt(KEY)
LOG2E = math.log2(math.e)

f32 = jnp.float32
bf16 = jnp.bfloat16
MIB = 1 << 20


def nn(left, right):
    return jnp.dot(left, right, preferred_element_type=f32)


def nt(left, right):
    return lax.dot_general(left, right, (((1,), (1,)), ((), ())), preferred_element_type=f32)


def call(kernel, outs, *args, scratch=(), flops=0, vmem=32, hbm=()):
    size = sum(math.prod(a.shape) * a.dtype.itemsize for a in args)
    return pl.pallas_call(
        kernel,
        out_shape=[jax.ShapeDtypeStruct(shape, kind) for shape, kind in outs],
        in_specs=[
            pl.BlockSpec(memory_space=pl.ANY if i in hbm else pltpu.VMEM) for i in range(len(args))
        ],
        out_specs=[pl.BlockSpec(memory_space=pltpu.VMEM)] * len(outs),
        scratch_shapes=list(scratch),
        compiler_params=pltpu.CompilerParams(vmem_limit_bytes=vmem * MIB),
        cost_estimate=pl.CostEstimate(flops=int(flops), bytes_accessed=int(size), transcendentals=0),
    )(*args)


def own_chip():
    section = lax.axis_index("section")
    return section >> 1, section & 1


def block_at(index, width):
    return pl.ds(pl.multiple_of(index * width, width), width)


def one_hot(marks):
    shape = (128, 32)
    spread = lax.broadcasted_iota(jnp.int32, shape, 0) >> 2 == lax.broadcasted_iota(jnp.int32, shape, 1)
    spread = jnp.where(spread, 1.0, 0.0).astype(bf16)
    wide = nn(spread, marks.astype(f32).astype(bf16))
    letter = (lax.broadcasted_iota(jnp.int32, wide.shape, 0) & 3).astype(f32)
    return jnp.where(wide == letter, 1.0, 0.0).T.astype(bf16)


def gelu(x):
    return jax.nn.gelu(x, approximate=True)


def stem_kernel(marks_ref, stem_ref, weight_hbm, act_ref, weight_ref, arrived):
    copy = pltpu.make_async_copy(weight_hbm, weight_ref, arrived)
    copy.start()
    hot = one_hot(marks_ref[...])
    for j in range(0, stem_ref.shape[1], 256):
        act_ref[:, j : j + 256] = gelu(nn(hot, stem_ref[:, j : j + 256])).astype(bf16)
    copy.wait()


def conv_kernel(marks_ref, low_ref, high_ref, stem_ref, act_ref, weight_ref, hidden_ref, ext_ref):
    rows = act_ref.shape[0]
    section = lax.axis_index("section")
    edge = one_hot(jnp.concatenate([low_ref[:, rows - HALO :], high_ref[:, :HALO]], axis=1))
    edge_act = gelu(nn(edge, stem_ref[...])).astype(bf16)
    ext_ref[0:HALO] = jnp.where(section > 0, edge_act[:HALO], 0)
    ext_ref[HALO : HALO + rows] = act_ref[...]
    ext_ref[HALO + rows :] = jnp.where(section < 3, edge_act[HALO:], 0)
    total = nn(one_hot(marks_ref[...]), stem_ref[:, block_at(lax.axis_index("tensor"), 384)])
    for k in range(3):
        total = total + nn(ext_ref[k * HALO : k * HALO + rows], weight_ref[k])
    hidden_ref[...] = total.astype(bf16)


def turn_kernel(q_ref, k_ref, v_ref, out_ref):
    out_ref[0:128] = q_ref[...].T
    out_ref[128:256] = k_ref[...].T
    out_ref[256:640] = v_ref[...].T


def taps_kernel(ext_ref, mine_ref, other_ref, turned):
    rows = turned.shape[1]
    _, core = own_chip()
    for k in range(3):
        turned[...] = ext_ref[k * HALO : k * HALO + rows].T
        for x in range(4):
            for z in range(4):
                to = ((x * 4 + z) * 3 + k) * 48
                base = z * 384 + x * 96
                mine_ref[to : to + 48] = turned[pl.ds(pl.multiple_of(base + core * 48, 16), 48)]
                other_ref[to : to + 48] = turned[
                    pl.ds(pl.multiple_of(base + (1 - core) * 48, 16), 48)
                ]


def distances():
    core = lax.axis_index("section") & 1
    return 1 + 2 * core, 3 - 2 * core


def gathered(blocks):
    own, first, second, far = blocks
    one, two = distances()
    return (0, own), (one, first), (two, second), (2, far)


def project_part_kernel(own, second, w_ref, out_ref):
    y = lax.axis_index("tensor")
    _, two = distances()
    out_ref[...] = nt(w_ref[:, block_at(y, 384)], own[...]) + nt(
        w_ref[:, block_at(y ^ two, 384)], second[...]
    )


def project_kernel(part, first, far, w_ref, mine_ref, other_ref, unit_ref, factor_ref, values):
    y = lax.axis_index("tensor")
    chip, _ = own_chip()
    one, _ = distances()
    total = part[...]
    for d, ref in ((one, first), (2, far)):
        total = total + nt(w_ref[:, block_at(y ^ d, 384)], ref[...])
    for g in range(4):
        raw = total[g * KEY : (g + 1) * KEY]
        factor = lax.rsqrt(jnp.mean(raw * raw, axis=0, keepdims=True) + EPSILON)
        unit_ref[g * KEY : (g + 1) * KEY] = raw * factor
        factor_ref[g : g + 1] = factor
    values[...] = total[256:].astype(bf16)
    for ref, head in ((mine_ref, chip), (other_ref, 1 - chip)):
        ref[0:64] = unit_ref[block_at(head, KEY)].astype(bf16)
        ref[64:128] = unit_ref[pl.ds(pl.multiple_of(128 + head * KEY, KEY), KEY)].astype(bf16)
        ref[128:320] = values[block_at(head, VAL)]


def grad_kernel(c0, c1, c2, c3, w_ref, mine_ref, other_ref):
    y = lax.axis_index("tensor")
    chip, _ = own_chip()
    for ref, head in ((mine_ref, chip), (other_ref, 1 - chip)):
        total = 0.0
        for d, block in gathered((c0, c1, c2, c3)):
            total = total + nt(w_ref[block_at(head, VAL), block_at(y ^ d, 384)], block[...])
        ref[...] = total.astype(bf16)


def attend_kernel(
    own, par, sib_own, sib_par, g_own, g_par,
    q_own_ref, q_par_ref, kv_mine_ref, kv_sib_ref,
    kv_t, kv_n, exps, score_grads, grads, queries,
):
    sections = (own, par, sib_own, sib_par)
    n = own.shape[1]
    for i, ref in enumerate(sections):
        kv = ref[64:320]
        kv_t[:, i * n : (i + 1) * n] = kv
        kv_n[i * n : (i + 1) * n] = kv.T
    width = 256
    zeros_q = jnp.zeros((VAL, width), bf16)
    zeros_g = jnp.zeros((KEY, width), bf16)
    for b in range(2 * n // width):
        src, g_src, dst = ((own, g_own, q_own_ref), (par, g_par, q_par_ref))[b * width // n]
        cols = slice((b * width) % n, (b * width) % n + width)
        lanes = slice(b * width, (b + 1) * width)
        query = src[0:64, cols]
        queries[:, lanes] = query
        right = jnp.concatenate([query, zeros_q], axis=0)
        total = jnp.zeros((1, width), f32)
        for i in range(4):
            e = jnp.exp2(nn(kv_n[i * n : (i + 1) * n], right) * (SCALE * LOG2E))
            total = total + jnp.sum(e, axis=0, keepdims=True)
            exps[i * n : (i + 1) * n, lanes] = e.astype(bf16)
        out = nn(kv_t[64:256], exps[:, lanes])
        inverse = 1.0 / total
        grad = (g_src[:, cols].astype(f32) * inverse).astype(bf16)
        grads[:, lanes] = grad
        inner = jnp.sum(grad.astype(f32) * out, axis=0, keepdims=True) * inverse
        right = jnp.concatenate([zeros_g, grad], axis=0)
        for i in range(4):
            prob = nn(kv_n[i * n : (i + 1) * n], right)
            e = exps[i * n : (i + 1) * n, lanes].astype(f32)
            score_grads[i * n : (i + 1) * n, lanes] = (e * (prob - inner)).astype(bf16)
        dst[:, cols] = (nn(kv_t[0:64], score_grads[:, lanes]) * SCALE).astype(bf16)
    for i, ref, at in ((2, kv_sib_ref, 0), (3, kv_sib_ref, n), (0, kv_mine_ref, 0), (1, kv_mine_ref, n)):
        key_grad = nt(queries[...], score_grads[i * n : (i + 1) * n]) * SCALE
        ref[0:64, at : at + n] = key_grad.astype(ref.dtype)
        value_grad = nt(grads[...], exps[i * n : (i + 1) * n])
        ref[64:256, at : at + n] = value_grad.astype(ref.dtype)


def join_kernel(q_own, q_par, kv_mine, kv_got, own_ref, par_ref):
    n = q_own.shape[1]
    par_ref[0:64] = q_par[...]
    par_ref[64:320] = (kv_mine[:, n:] + kv_got[:, n:].astype(f32)).astype(bf16)
    own_ref[0:64] = q_own[...]
    own_ref[64:320] = (kv_mine[:, :n] + kv_got[:, :n].astype(f32)).astype(bf16)


def back_kernel(own, other, unit_ref, factor_ref, wq, wk, wv, back, far_ref):
    y = lax.axis_index("tensor")
    chip, _ = own_chip()
    for ref, head in ((own, chip), (other, 1 - chip)):
        for kind in range(2):
            at = pl.ds(pl.multiple_of(kind * 128 + head * KEY, KEY), KEY)
            unit = unit_ref[at]
            factor = factor_ref[pl.ds(kind * 2 + head, 1)]
            g = ref[kind * 64 : kind * 64 + 64].astype(f32)
            mean = jnp.mean(g * unit, axis=0, keepdims=True)
            back[at] = (factor * (g - unit * mean)).astype(bf16)
        back[pl.ds(pl.multiple_of(256 + head * VAL, 64), VAL)] = ref[128:320]
    far_ref[...] = back_rows(back, wq, wk, wv, y ^ 2).astype(bf16)


def back_rows(back, wq, wk, wv, index):
    at = block_at(index, 384)
    qk = jnp.concatenate([wq[at], wk[at]], axis=1)
    return nn(qk, back[0:256]) + nn(wv[at], back[256:640])


def back_near_kernel(back, wq, wk, wv, alone_ref, joined_ref):
    y = lax.axis_index("tensor")
    one, two = distances()
    alone_ref[...] = back_rows(back, wq, wk, wv, y ^ one).astype(bf16)
    joined_ref[...] = back_rows(back, wq, wk, wv, y ^ two)


def back_own_kernel(back, wq, wk, wv, cot, out_ref):
    y = lax.axis_index("tensor")
    out_ref[...] = back_rows(back, wq, wk, wv, y) + cot[...].astype(f32).T


def add_kernel(joined, got, out_ref):
    out_ref[...] = (joined[...] + got[...].astype(f32)).astype(bf16)


def hidden_grad_kernel(own, alone, joined, out_ref):
    out_ref[...] = (own[...] + alone[...].astype(f32) + joined[...].astype(f32)).astype(bf16)


def ring_place():
    x = (lax.axis_index("seq") & 1) * 2 + (lax.axis_index("section") >> 1)
    z = lax.axis_index("seq") >> 1
    return x, z


def tap_own_kernel(taps, grad, out_ref):
    x, _ = ring_place()
    for i, d in enumerate((2, distances()[0])):
        out_ref[i] = nt(taps[block_at(x ^ d, 576)], grad[...])


def tap_add_kernel(index, own, taps, grad, out_ref):
    x, _ = ring_place()
    d = (2, distances()[0])[index]
    out_ref[...] = (own[index] + nt(taps[block_at(x ^ d, 576)], grad[...])).astype(bf16)


def tap_kernel(which, t_mine, t_sib, g_mine, g_sib, out_ref):
    x, _ = ring_place()
    d = (0, *distances(), 2)[which]
    at = block_at(x ^ d, 576)
    out_ref[...] = (nt(t_mine[at], g_mine[...]) + nt(t_sib[at], g_sib[...])).astype(out_ref.dtype)


def sum_x_kernel(own, alone, joined, own_ref, to1, to2, to3):
    _, z = ring_place()
    for d, ref in ((2, to2), (1, to1), (3, to3), (0, own_ref)):
        at = block_at(z ^ d, 144)
        ref[...] = (own[at] + alone[at].astype(f32) + joined[at].astype(f32)).astype(ref.dtype)


def sum_z_kernel(norm, own, r1, r2, r3, out_ref):
    out_ref[...] = (
        own[...] + r1[...].astype(f32) + r2[...].astype(f32) + r3[...].astype(f32)
    ) * norm


def body(bases, stem_w, conv_w, wq, wk, wv, out_w, cot):
    marks = bases[0].T
    cot = cot[0]
    rows = marks.shape[1]
    flat = ("seq", "section")

    low = lax.ppermute(marks, "section", [(i, (i + 1) % 4) for i in range(4)])
    high = lax.ppermute(marks, "section", [((i + 1) % 4, i) for i in range(4)])

    def y_way(value, way):
        pairs = []
        for t in range(4):
            for i in range(4):
                pairs.append((t * 4 + i, (t ^ (1, 3)[(i + way) % 2]) * 4 + i))
        return lax.ppermute(value, ("tensor", "section"), pairs)

    def x_way(value, way):
        return lax.ppermute(value, flat, [(i, i ^ (2 * (1, 3)[(i + way) % 2])) for i in range(32)])

    def over_core(value):
        return lax.ppermute(value, "section", [(i, i ^ 1) for i in range(4)])

    def over_chip(value):
        return lax.ppermute(value, "section", [(i, i ^ 2) for i in range(4)])

    def over_z(value, d):
        return lax.ppermute(value, flat, [(i, i ^ (8 * d)) for i in range(32)])

    second = y_way(cot, 1)
    act, conv_here = call(
        stem_kernel, [((rows, 1536), bf16), (conv_w.shape, bf16)], marks, stem_w, conv_w,
        scratch=[pltpu.SemaphoreType.DMA(())], flops=4e8, vmem=16, hbm=(2,),
    )
    first = y_way(cot, 0)
    hidden, ext = call(
        conv_kernel,
        [((rows, 384), bf16), ((rows + 2 * HALO, 1536), bf16)],
        marks, low, high, stem_w, act, conv_here,
        flops=2e9,
    )
    far = y_way(second, 0)
    cots = (cot, first, second, far)

    second = y_way(hidden, 1)
    taps_mine, taps_other = call(
        taps_kernel, [((2304, rows), bf16)] * 2, ext,
        scratch=[pltpu.VMEM((1536, rows), bf16)], flops=3e9,
    )
    (w_t,) = call(turn_kernel, [((640, 1536), bf16)], wq, wk, wv, flops=1e9)
    first = y_way(lax.optimization_barrier((hidden, taps_mine, w_t))[0], 0)
    second, cots = lax.optimization_barrier((second, cots))
    far = y_way(second, 0)
    g_own, g_other = call(grad_kernel, [((VAL, rows), bf16)] * 2, *cots, out_w, flops=1e9)
    g_par = over_chip(g_other)
    (part,) = call(project_part_kernel, [((640, rows), f32)], hidden, second, w_t, flops=7e8)
    first, far, part = lax.optimization_barrier((first, far, part))

    own, other, unit, factor = call(
        project_kernel,
        [((320, rows), bf16)] * 2 + [((256, rows), f32), ((4, rows), f32)],
        part, first, far, w_t,
        scratch=[pltpu.VMEM((384, rows), bf16)], flops=1.5e9,
    )
    other, g_par, g_own = lax.optimization_barrier((other, g_par, g_own))
    par = over_chip(other)
    sib_own = over_core(own)
    sib_par = over_core(par)
    taps_sib = over_core(taps_other)
    q_own, q_par, kv_mine, kv_sib = call(
        attend_kernel,
        [((KEY, rows), bf16)] * 2 + [((256, 2 * rows), f32), ((256, 2 * rows), bf16)],
        own, par, sib_own, sib_par, g_own, g_par,
        scratch=[
            pltpu.VMEM((256, 4 * rows), bf16),
            pltpu.VMEM((4 * rows, 256), bf16),
            pltpu.VMEM((4 * rows, 2 * rows), bf16),
            pltpu.VMEM((4 * rows, 2 * rows), bf16),
            pltpu.VMEM((VAL, 2 * rows), bf16),
            pltpu.VMEM((KEY, 2 * rows), bf16),
        ],
        flops=8e9, vmem=48,
    )
    kv_got = over_core(kv_sib)
    back_own, back_par = call(join_kernel, [((320, rows), bf16)] * 2, q_own, q_par, kv_mine, kv_got)
    back_other = over_chip(back_par)
    back, far = call(
        back_kernel,
        [((640, rows), bf16), ((384, rows), bf16)],
        back_own, back_other, unit, factor, wq, wk, wv, flops=5e8,
    )
    got = y_way(far, 0)
    alone, joined = call(
        back_near_kernel, [((384, rows), bf16), ((384, rows), f32)], back, wq, wk, wv, flops=8e8
    )
    alone = y_way(alone, 0)
    (grad_own,) = call(back_own_kernel, [((384, rows), f32)], back, wq, wk, wv, cot, flops=5e8)
    (joined,) = call(add_kernel, [((384, rows), bf16)], joined, got)
    joined = y_way(joined, 1)
    (hg,) = call(hidden_grad_kernel, [((384, rows), bf16)], grad_own, alone, joined)
    hg_sib = over_core(hg)

    def product(which, kind):
        return call(
            functools.partial(tap_kernel, which),
            [((576, 384), kind)],
            taps_mine, taps_sib, hg, hg_sib, flops=6e8,
        )[0]

    (parts,) = call(tap_own_kernel, [((2, 576, 384), f32)], taps_mine, hg, flops=6e8)
    hg_sib, parts = lax.optimization_barrier((hg_sib, parts))
    far, near = [
        call(
            functools.partial(tap_add_kernel, i), [((576, 384), bf16)], parts, taps_sib, hg_sib, flops=3e8
        )[0]
        for i in range(2)
    ]
    got = x_way(far, 0)
    alone = x_way(near, 0)
    joined = product(2, f32)
    part = product(0, f32)
    (joined,) = call(add_kernel, [((576, 384), bf16)], joined, got)
    joined = x_way(joined, 1)
    own_z, z1, z2, z3 = call(
        sum_x_kernel, [((144, 384), f32)] + [((144, 384), bf16)] * 3, part, alone, joined
    )
    got = [over_z(z2, 2), over_z(z1, 1), over_z(z3, 3)]
    norm = 1.0 / math.sqrt(rows * 32)
    (total,) = call(functools.partial(sum_z_kernel, norm), [((144, 384), f32)], own_z, *got)
    return total.reshape(3, 48, 384).transpose(1, 0, 2)


def solution(mesh):
    in_specs = (
        P("seq", "section", None),
        P(),
        P(None, None, "tensor"),
        P(None, "tensor"),
        P(None, "tensor"),
        P(None, "tensor"),
        P("tensor", None),
        P("seq", "section", "tensor"),
    )
    out_specs = P(("seq", "section"), None, "tensor")
    return jax.shard_map(body, mesh=mesh, in_specs=in_specs, out_specs=out_specs, check_vma=False)
```

```python
import functools
import math

import jax
import jax.numpy as jnp
from jax import lax
from jax.experimental import pallas as pl
from jax.experimental.pallas import tpu as pltpu
from jax.sharding import PartitionSpec as P

KEY = 64
VAL = 192
HALO = 32
EPSILON = 1e-06
SCALE = 3.0 / math.sqrt(KEY)
LOG2E = math.log2(math.e)

f32 = jnp.float32
bf16 = jnp.bfloat16
MIB = 1 << 20


def nn(left, right):
    return jnp.dot(left, right, preferred_element_type=f32)


def nt(left, right):
    return lax.dot_general(left, right, (((1,), (1,)), ((), ())), preferred_element_type=f32)


def call(kernel, outs, *args, scratch=(), flops=0, vmem=32, hbm=()):
    size = sum(math.prod(a.shape) * a.dtype.itemsize for a in args)
    return pl.pallas_call(
        kernel,
        out_shape=[jax.ShapeDtypeStruct(shape, kind) for shape, kind in outs],
        in_specs=[
            pl.BlockSpec(memory_space=pl.ANY if i in hbm else pltpu.VMEM) for i in range(len(args))
        ],
        out_specs=[pl.BlockSpec(memory_space=pltpu.VMEM)] * len(outs),
        scratch_shapes=list(scratch),
        compiler_params=pltpu.CompilerParams(vmem_limit_bytes=vmem * MIB),
        cost_estimate=pl.CostEstimate(flops=int(flops), bytes_accessed=int(size), transcendentals=0),
    )(*args)


def own_chip():
    section = lax.axis_index("section")
    return section >> 1, section & 1


def block_at(index, width):
    return pl.ds(pl.multiple_of(index * width, width), width)


def one_hot(marks):
    shape = (128, 32)
    spread = lax.broadcasted_iota(jnp.int32, shape, 0) >> 2 == lax.broadcasted_iota(jnp.int32, shape, 1)
    spread = jnp.where(spread, 1.0, 0.0).astype(bf16)
    wide = nn(spread, marks.astype(f32).astype(bf16))
    letter = (lax.broadcasted_iota(jnp.int32, wide.shape, 0) & 3).astype(f32)
    return jnp.where(wide == letter, 1.0, 0.0).T.astype(bf16)


def gelu(x):
    return jax.nn.gelu(x, approximate=True)


def stem_kernel(marks_ref, stem_ref, act_ref):
    hot = one_hot(marks_ref[...])
    for j in range(0, stem_ref.shape[1], 256):
        act_ref[:, j : j + 256] = gelu(nn(hot, stem_ref[:, j : j + 256])).astype(bf16)


def conv_kernel(marks_ref, low_ref, high_ref, stem_ref, act_ref, weight_ref, hidden_ref, ext_ref):
    rows = act_ref.shape[0]
    section = lax.axis_index("section")
    edge = one_hot(jnp.concatenate([low_ref[:, rows - HALO :], high_ref[:, :HALO]], axis=1))
    edge_act = gelu(nn(edge, stem_ref[...])).astype(bf16)
    ext_ref[0:HALO] = jnp.where(section > 0, edge_act[:HALO], 0)
    ext_ref[HALO : HALO + rows] = act_ref[...]
    ext_ref[HALO + rows :] = jnp.where(section < 3, edge_act[HALO:], 0)
    total = nn(one_hot(marks_ref[...]), stem_ref[:, block_at(lax.axis_index("tensor"), 384)])
    for k in range(3):
        total = total + nn(ext_ref[k * HALO : k * HALO + rows], weight_ref[k])
    hidden_ref[...] = total.astype(bf16)


def turn_kernel(q_ref, k_ref, v_ref, out_ref):
    out_ref[0:128] = q_ref[...].T
    out_ref[128:256] = k_ref[...].T
    out_ref[256:640] = v_ref[...].T


def taps_kernel(ext_ref, mine_ref, other_ref, turned):
    rows = turned.shape[1]
    _, core = own_chip()
    for k in range(3):
        turned[...] = ext_ref[k * HALO : k * HALO + rows].T
        for x in range(4):
            for z in range(4):
                to = ((x * 4 + z) * 3 + k) * 48
                base = z * 384 + x * 96
                mine_ref[to : to + 48] = turned[pl.ds(pl.multiple_of(base + core * 48, 16), 48)]
                other_ref[to : to + 48] = turned[
                    pl.ds(pl.multiple_of(base + (1 - core) * 48, 16), 48)
                ]


def distances():
    core = lax.axis_index("section") & 1
    return 1 + 2 * core, 3 - 2 * core


def gathered(blocks):
    own, first, second, far = blocks
    one, two = distances()
    return (0, own), (one, first), (two, second), (2, far)


def project_part_kernel(own, second, w_ref, out_ref):
    y = lax.axis_index("tensor")
    _, two = distances()
    out_ref[...] = nt(w_ref[:, block_at(y, 384)], own[...]) + nt(
        w_ref[:, block_at(y ^ two, 384)], second[...]
    )


def project_kernel(part, first, far, w_ref, mine_ref, other_ref, unit_ref, factor_ref, values):
    y = lax.axis_index("tensor")
    chip, _ = own_chip()
    one, _ = distances()
    total = part[...]
    for d, ref in ((one, first), (2, far)):
        total = total + nt(w_ref[:, block_at(y ^ d, 384)], ref[...])
    for g in range(4):
        raw = total[g * KEY : (g + 1) * KEY]
        factor = lax.rsqrt(jnp.mean(raw * raw, axis=0, keepdims=True) + EPSILON)
        unit_ref[g * KEY : (g + 1) * KEY] = raw * factor
        factor_ref[g : g + 1] = factor
    values[...] = total[256:].astype(bf16)
    for ref, head in ((mine_ref, chip), (other_ref, 1 - chip)):
        ref[0:64] = unit_ref[block_at(head, KEY)].astype(bf16)
        ref[64:128] = unit_ref[pl.ds(pl.multiple_of(128 + head * KEY, KEY), KEY)].astype(bf16)
        ref[128:320] = values[block_at(head, VAL)]


def grad_kernel(c0, c1, c2, c3, w_ref, mine_ref, other_ref):
    y = lax.axis_index("tensor")
    chip, _ = own_chip()
    for ref, head in ((mine_ref, chip), (other_ref, 1 - chip)):
        total = 0.0
        for d, block in gathered((c0, c1, c2, c3)):
            total = total + nt(w_ref[block_at(head, VAL), block_at(y ^ d, 384)], block[...])
        ref[...] = total.astype(bf16)


def attend_kernel(
    own, par, sib_own, sib_par, g_own, g_par,
    q_own_ref, q_par_ref, kv_mine_ref, kv_sib_ref,
    kv_t, kv_n, exps, score_grads, grads, queries,
):
    sections = (own, par, sib_own, sib_par)
    n = own.shape[1]
    for i, ref in enumerate(sections):
        kv = ref[64:320]
        kv_t[:, i * n : (i + 1) * n] = kv
        kv_n[i * n : (i + 1) * n] = kv.T
    width = 256
    zeros_q = jnp.zeros((VAL, width), bf16)
    zeros_g = jnp.zeros((KEY, width), bf16)
    for b in range(2 * n // width):
        src, g_src, dst = ((own, g_own, q_own_ref), (par, g_par, q_par_ref))[b * width // n]
        cols = slice((b * width) % n, (b * width) % n + width)
        lanes = slice(b * width, (b + 1) * width)
        query = src[0:64, cols]
        queries[:, lanes] = query
        right = jnp.concatenate([query, zeros_q], axis=0)
        total = jnp.zeros((1, width), f32)
        for i in range(4):
            e = jnp.exp2(nn(kv_n[i * n : (i + 1) * n], right) * (SCALE * LOG2E))
            total = total + jnp.sum(e, axis=0, keepdims=True)
            exps[i * n : (i + 1) * n, lanes] = e.astype(bf16)
        out = nn(kv_t[64:256], exps[:, lanes])
        inverse = 1.0 / total
        grad = (g_src[:, cols].astype(f32) * inverse).astype(bf16)
        grads[:, lanes] = grad
        inner = jnp.sum(grad.astype(f32) * out, axis=0, keepdims=True) * inverse
        right = jnp.concatenate([zeros_g, grad], axis=0)
        for i in range(4):
            prob = nn(kv_n[i * n : (i + 1) * n], right)
            e = exps[i * n : (i + 1) * n, lanes].astype(f32)
            score_grads[i * n : (i + 1) * n, lanes] = (e * (prob - inner)).astype(bf16)
        dst[:, cols] = (nn(kv_t[0:64], score_grads[:, lanes]) * SCALE).astype(bf16)
    for i, ref, at in ((2, kv_sib_ref, 0), (3, kv_sib_ref, n), (0, kv_mine_ref, 0), (1, kv_mine_ref, n)):
        key_grad = nt(queries[...], score_grads[i * n : (i + 1) * n]) * SCALE
        ref[0:64, at : at + n] = key_grad.astype(ref.dtype)
        value_grad = nt(grads[...], exps[i * n : (i + 1) * n])
        ref[64:256, at : at + n] = value_grad.astype(ref.dtype)


def join_kernel(q_own, q_par, kv_mine, kv_got, own_ref, par_ref):
    n = q_own.shape[1]
    par_ref[0:64] = q_par[...]
    par_ref[64:320] = (kv_mine[:, n:] + kv_got[:, n:].astype(f32)).astype(bf16)
    own_ref[0:64] = q_own[...]
    own_ref[64:320] = (kv_mine[:, :n] + kv_got[:, :n].astype(f32)).astype(bf16)


def back_kernel(own, other, unit_ref, factor_ref, wq, wk, wv, back, far_ref):
    y = lax.axis_index("tensor")
    chip, _ = own_chip()
    for ref, head in ((own, chip), (other, 1 - chip)):
        for kind in range(2):
            at = pl.ds(pl.multiple_of(kind * 128 + head * KEY, KEY), KEY)
            unit = unit_ref[at]
            factor = factor_ref[pl.ds(kind * 2 + head, 1)]
            g = ref[kind * 64 : kind * 64 + 64].astype(f32)
            mean = jnp.mean(g * unit, axis=0, keepdims=True)
            back[at] = (factor * (g - unit * mean)).astype(bf16)
        back[pl.ds(pl.multiple_of(256 + head * VAL, 64), VAL)] = ref[128:320]
    far_ref[...] = back_rows(back, wq, wk, wv, y ^ 2).astype(bf16)


def back_rows(back, wq, wk, wv, index):
    at = block_at(index, 384)
    qk = jnp.concatenate([wq[at], wk[at]], axis=1)
    return nn(qk, back[0:256]) + nn(wv[at], back[256:640])


def back_near_kernel(back, wq, wk, wv, alone_ref, joined_ref):
    y = lax.axis_index("tensor")
    one, two = distances()
    alone_ref[...] = back_rows(back, wq, wk, wv, y ^ one).astype(bf16)
    joined_ref[...] = back_rows(back, wq, wk, wv, y ^ two)


def back_own_kernel(back, wq, wk, wv, cot, out_ref):
    y = lax.axis_index("tensor")
    out_ref[...] = back_rows(back, wq, wk, wv, y) + cot[...].astype(f32).T


def add_kernel(joined, got, out_ref):
    out_ref[...] = (joined[...] + got[...].astype(f32)).astype(bf16)


def hidden_grad_kernel(own, alone, joined, out_ref):
    out_ref[...] = (own[...] + alone[...].astype(f32) + joined[...].astype(f32)).astype(bf16)


def ring_place():
    x = (lax.axis_index("seq") & 1) * 2 + (lax.axis_index("section") >> 1)
    z = lax.axis_index("seq") >> 1
    return x, z


def tap_own_kernel(taps, grad, out_ref):
    x, _ = ring_place()
    for i, d in enumerate((2, distances()[0])):
        out_ref[i] = nt(taps[block_at(x ^ d, 576)], grad[...])


def tap_add_kernel(index, own, taps, grad, out_ref):
    x, _ = ring_place()
    d = (2, distances()[0])[index]
    out_ref[...] = (own[index] + nt(taps[block_at(x ^ d, 576)], grad[...])).astype(bf16)


def tap_kernel(which, t_mine, t_sib, g_mine, g_sib, out_ref):
    x, _ = ring_place()
    d = (0, *distances(), 2)[which]
    at = block_at(x ^ d, 576)
    out_ref[...] = (nt(t_mine[at], g_mine[...]) + nt(t_sib[at], g_sib[...])).astype(out_ref.dtype)


def sum_x_kernel(own, alone, joined, own_ref, to1, to2, to3):
    _, z = ring_place()
    for d, ref in ((2, to2), (1, to1), (3, to3), (0, own_ref)):
        at = block_at(z ^ d, 144)
        ref[...] = (own[at] + alone[at].astype(f32) + joined[at].astype(f32)).astype(ref.dtype)


def sum_z_kernel(norm, own, r1, r2, r3, out_ref):
    out_ref[...] = (
        own[...] + r1[...].astype(f32) + r2[...].astype(f32) + r3[...].astype(f32)
    ) * norm


def body(bases, stem_w, conv_w, wq, wk, wv, out_w, cot):
    marks = bases[0].T
    cot = cot[0]
    rows = marks.shape[1]
    flat = ("seq", "section")

    low = lax.ppermute(marks, "section", [(i, (i + 1) % 4) for i in range(4)])
    high = lax.ppermute(marks, "section", [((i + 1) % 4, i) for i in range(4)])

    def y_way(value, way):
        pairs = []
        for t in range(4):
            for i in range(4):
                pairs.append((t * 4 + i, (t ^ (1, 3)[(i + way) % 2]) * 4 + i))
        return lax.ppermute(value, ("tensor", "section"), pairs)

    def x_way(value, way):
        return lax.ppermute(value, flat, [(i, i ^ (2 * (1, 3)[(i + way) % 2])) for i in range(32)])

    def over_core(value):
        return lax.ppermute(value, "section", [(i, i ^ 1) for i in range(4)])

    def over_chip(value):
        return lax.ppermute(value, "section", [(i, i ^ 2) for i in range(4)])

    def over_z(value, d):
        return lax.ppermute(value, flat, [(i, i ^ (8 * d)) for i in range(32)])

    second = y_way(cot, 1)
    (act,) = call(stem_kernel, [((rows, 1536), bf16)], marks, stem_w, flops=4e9, vmem=16)
    first = y_way(cot, 0)
    hidden, ext = call(
        conv_kernel,
        [((rows, 384), bf16), ((rows + 2 * HALO, 1536), bf16)],
        marks, low, high, stem_w, act, conv_w,
        flops=2e9,
    )
    cots = [cot, first, second]

    second = y_way(hidden, 1)
    taps_mine, taps_other = call(
        taps_kernel, [((2304, rows), bf16)] * 2, ext,
        scratch=[pltpu.VMEM((1536, rows), bf16)], flops=3e9,
    )
    _, wv_late = lax.optimization_barrier((hidden, wv))
    (w_t,) = call(turn_kernel, [((640, 1536), bf16)], wq, wk, wv_late, flops=1e9)
    tied, cots, taps_mine, w_t = lax.optimization_barrier((hidden, cots, taps_mine, w_t))
    cots = cots + [y_way(cots[2], 0)]
    first = y_way(tied, 0)
    second, cots = lax.optimization_barrier((second, cots))
    far = y_way(second, 0)
    g_own, g_other = call(grad_kernel, [((VAL, rows), bf16)] * 2, *cots, out_w, flops=1e9)
    g_par = over_chip(g_other)
    (part,) = call(project_part_kernel, [((640, rows), f32)], hidden, second, w_t, flops=7e8)
    first, far, part = lax.optimization_barrier((first, far, part))

    own, other, unit, factor = call(
        project_kernel,
        [((320, rows), bf16)] * 2 + [((256, rows), f32), ((4, rows), f32)],
        part, first, far, w_t,
        scratch=[pltpu.VMEM((384, rows), bf16)], flops=1.5e9,
    )
    other, g_par, g_own = lax.optimization_barrier((other, g_par, g_own))
    par = over_chip(other)
    sib_own = over_core(own)
    sib_par = over_core(par)
    taps_sib = over_core(taps_other)
    q_own, q_par, kv_mine, kv_sib = call(
        attend_kernel,
        [((KEY, rows), bf16)] * 2 + [((256, 2 * rows), f32), ((256, 2 * rows), bf16)],
        own, par, sib_own, sib_par, g_own, g_par,
        scratch=[
            pltpu.VMEM((256, 4 * rows), bf16),
            pltpu.VMEM((4 * rows, 256), bf16),
            pltpu.VMEM((4 * rows, 2 * rows), bf16),
            pltpu.VMEM((4 * rows, 2 * rows), bf16),
            pltpu.VMEM((VAL, 2 * rows), bf16),
            pltpu.VMEM((KEY, 2 * rows), bf16),
        ],
        flops=8e9, vmem=48,
    )
    kv_got = over_core(kv_sib)
    back_own, back_par = call(join_kernel, [((320, rows), bf16)] * 2, q_own, q_par, kv_mine, kv_got)
    back_other = over_chip(back_par)
    back, far = call(
        back_kernel,
        [((640, rows), bf16), ((384, rows), bf16)],
        back_own, back_other, unit, factor, wq, wk, wv, flops=5e8,
    )
    got = y_way(far, 0)
    alone, joined = call(
        back_near_kernel, [((384, rows), bf16), ((384, rows), f32)], back, wq, wk, wv, flops=8e8
    )
    alone = y_way(alone, 0)
    (grad_own,) = call(back_own_kernel, [((384, rows), f32)], back, wq, wk, wv, cot, flops=5e8)
    (joined,) = call(add_kernel, [((384, rows), bf16)], joined, got)
    joined = y_way(joined, 1)
    (hg,) = call(hidden_grad_kernel, [((384, rows), bf16)], grad_own, alone, joined)
    hg_sib = over_core(hg)

    def product(which, kind):
        return call(
            functools.partial(tap_kernel, which),
            [((576, 384), kind)],
            taps_mine, taps_sib, hg, hg_sib, flops=6e8,
        )[0]

    (parts,) = call(tap_own_kernel, [((2, 576, 384), f32)], taps_mine, hg, flops=6e8)
    hg_sib, parts = lax.optimization_barrier((hg_sib, parts))
    far, near = [
        call(
            functools.partial(tap_add_kernel, i), [((576, 384), bf16)], parts, taps_sib, hg_sib, flops=3e8
        )[0]
        for i in range(2)
    ]
    got = x_way(far, 0)
    alone = x_way(near, 0)
    joined = product(2, f32)
    part = product(0, f32)
    (joined,) = call(add_kernel, [((576, 384), bf16)], joined, got)
    joined = x_way(joined, 1)
    own_z, z1, z2, z3 = call(
        sum_x_kernel, [((144, 384), f32)] + [((144, 384), bf16)] * 3, part, alone, joined
    )
    got = [over_z(z2, 2), over_z(z1, 1), over_z(z3, 3)]
    norm = 1.0 / math.sqrt(rows * 32)
    (total,) = call(functools.partial(sum_z_kernel, norm), [((144, 384), f32)], own_z, *got)
    return total.reshape(3, 48, 384).transpose(1, 0, 2)


def solution(mesh):
    in_specs = (
        P("seq", "section", None),
        P(),
        P(None, None, "tensor"),
        P(None, "tensor"),
        P(None, "tensor"),
        P(None, "tensor"),
        P("tensor", None),
        P("seq", "section", "tensor"),
    )
    out_specs = P(("seq", "section"), None, "tensor")
    return jax.shard_map(body, mesh=mesh, in_specs=in_specs, out_specs=out_specs, check_vma=False)
```

```python
import functools
import math

import jax
import jax.numpy as jnp
from jax import lax
from jax.experimental import pallas as pl
from jax.experimental.pallas import tpu as pltpu
from jax.sharding import PartitionSpec as P

KEY = 64
VAL = 192
HALO = 32
EPSILON = 1e-06
SCALE = 3.0 / math.sqrt(KEY)
LOG2E = math.log2(math.e)

f32 = jnp.float32
bf16 = jnp.bfloat16
MIB = 1 << 20


def nn(left, right):
    return jnp.dot(left, right, preferred_element_type=f32)


def nt(left, right):
    return lax.dot_general(left, right, (((1,), (1,)), ((), ())), preferred_element_type=f32)


def call(kernel, outs, *args, scratch=(), flops=0, vmem=32, hbm=()):
    size = sum(math.prod(a.shape) * a.dtype.itemsize for a in args)
    return pl.pallas_call(
        kernel,
        out_shape=[jax.ShapeDtypeStruct(shape, kind) for shape, kind in outs],
        in_specs=[
            pl.BlockSpec(memory_space=pl.ANY if i in hbm else pltpu.VMEM) for i in range(len(args))
        ],
        out_specs=[pl.BlockSpec(memory_space=pltpu.VMEM)] * len(outs),
        scratch_shapes=list(scratch),
        compiler_params=pltpu.CompilerParams(vmem_limit_bytes=vmem * MIB),
        cost_estimate=pl.CostEstimate(flops=int(flops), bytes_accessed=int(size), transcendentals=0),
    )(*args)


def own_chip():
    section = lax.axis_index("section")
    return section >> 1, section & 1


def block_at(index, width):
    return pl.ds(pl.multiple_of(index * width, width), width)


def one_hot(marks):
    shape = (128, 32)
    spread = lax.broadcasted_iota(jnp.int32, shape, 0) >> 2 == lax.broadcasted_iota(jnp.int32, shape, 1)
    spread = jnp.where(spread, 1.0, 0.0).astype(bf16)
    wide = nn(spread, marks.astype(f32).astype(bf16))
    letter = (lax.broadcasted_iota(jnp.int32, wide.shape, 0) & 3).astype(f32)
    return jnp.where(wide == letter, 1.0, 0.0).T.astype(bf16)


def gelu(x):
    return jax.nn.gelu(x, approximate=True)


def stem_kernel(marks_ref, stem_ref, act_ref):
    hot = one_hot(marks_ref[...])
    for j in range(0, stem_ref.shape[1], 256):
        act_ref[:, j : j + 256] = gelu(nn(hot, stem_ref[:, j : j + 256])).astype(bf16)


def conv_kernel(marks_ref, low_ref, high_ref, stem_ref, act_ref, weight_ref, hidden_ref, ext_ref):
    rows = act_ref.shape[0]
    section = lax.axis_index("section")
    edge = one_hot(jnp.concatenate([low_ref[:, rows - HALO :], high_ref[:, :HALO]], axis=1))
    edge_act = gelu(nn(edge, stem_ref[...])).astype(bf16)
    ext_ref[0:HALO] = jnp.where(section > 0, edge_act[:HALO], 0)
    ext_ref[HALO : HALO + rows] = act_ref[...]
    ext_ref[HALO + rows :] = jnp.where(section < 3, edge_act[HALO:], 0)
    total = nn(one_hot(marks_ref[...]), stem_ref[:, block_at(lax.axis_index("tensor"), 384)])
    for k in range(3):
        total = total + nn(ext_ref[k * HALO : k * HALO + rows], weight_ref[k])
    hidden_ref[...] = total.astype(bf16)


def turn_kernel(q_ref, k_ref, v_ref, out_ref):
    out_ref[0:128] = q_ref[...].T
    out_ref[128:256] = k_ref[...].T
    out_ref[256:640] = v_ref[...].T


def taps_kernel(ext_ref, mine_ref, other_ref, turned):
    rows = turned.shape[1]
    _, core = own_chip()
    for k in range(3):
        turned[...] = ext_ref[k * HALO : k * HALO + rows].T
        for x in range(4):
            for z in range(4):
                to = ((x * 4 + z) * 3 + k) * 48
                base = z * 384 + x * 96
                mine_ref[to : to + 48] = turned[pl.ds(pl.multiple_of(base + core * 48, 16), 48)]
                other_ref[to : to + 48] = turned[
                    pl.ds(pl.multiple_of(base + (1 - core) * 48, 16), 48)
                ]


def distances():
    core = lax.axis_index("section") & 1
    return 1 + 2 * core, 3 - 2 * core


def gathered(blocks):
    own, first, second, far = blocks
    one, two = distances()
    return (0, own), (one, first), (two, second), (2, far)


def project_part_kernel(own, second, w_ref, out_ref):
    y = lax.axis_index("tensor")
    _, two = distances()
    out_ref[...] = nt(w_ref[:, block_at(y, 384)], own[...]) + nt(
        w_ref[:, block_at(y ^ two, 384)], second[...]
    )


def project_kernel(part, first, far, w_ref, mine_ref, other_ref, unit_ref, factor_ref, values):
    y = lax.axis_index("tensor")
    chip, _ = own_chip()
    one, _ = distances()
    total = part[...]
    for d, ref in ((one, first), (2, far)):
        total = total + nt(w_ref[:, block_at(y ^ d, 384)], ref[...])
    for g in range(4):
        raw = total[g * KEY : (g + 1) * KEY]
        factor = lax.rsqrt(jnp.mean(raw * raw, axis=0, keepdims=True) + EPSILON)
        unit_ref[g * KEY : (g + 1) * KEY] = raw * factor
        factor_ref[g : g + 1] = factor
    values[...] = total[256:].astype(bf16)
    for ref, head in ((mine_ref, chip), (other_ref, 1 - chip)):
        ref[0:64] = unit_ref[block_at(head, KEY)].astype(bf16)
        ref[64:128] = unit_ref[pl.ds(pl.multiple_of(128 + head * KEY, KEY), KEY)].astype(bf16)
        ref[128:320] = values[block_at(head, VAL)]


def grad_kernel(c0, c1, c2, c3, w_ref, mine_ref, other_ref):
    y = lax.axis_index("tensor")
    chip, _ = own_chip()
    for ref, head in ((mine_ref, chip), (other_ref, 1 - chip)):
        total = 0.0
        for d, block in gathered((c0, c1, c2, c3)):
            total = total + nt(w_ref[block_at(head, VAL), block_at(y ^ d, 384)], block[...])
        ref[...] = total.astype(bf16)


def attend_kernel(
    own, par, sib_own, sib_par, g_own, g_par,
    q_own_ref, q_par_ref, kv_mine_ref, kv_sib_ref,
    kv_t, kv_n, exps, score_grads, grads, queries,
):
    sections = (own, par, sib_own, sib_par)
    n = own.shape[1]
    for i, ref in enumerate(sections):
        kv = ref[64:320]
        kv_t[:, i * n : (i + 1) * n] = kv
        kv_n[i * n : (i + 1) * n] = kv.T
    width = 256
    zeros_q = jnp.zeros((VAL, width), bf16)
    zeros_g = jnp.zeros((KEY, width), bf16)
    for b in range(2 * n // width):
        src, g_src, dst = ((own, g_own, q_own_ref), (par, g_par, q_par_ref))[b * width // n]
        cols = slice((b * width) % n, (b * width) % n + width)
        lanes = slice(b * width, (b + 1) * width)
        query = src[0:64, cols]
        queries[:, lanes] = query
        right = jnp.concatenate([query, zeros_q], axis=0)
        total = jnp.zeros((1, width), f32)
        for i in range(4):
            e = jnp.exp2(nn(kv_n[i * n : (i + 1) * n], right) * (SCALE * LOG2E))
            total = total + jnp.sum(e, axis=0, keepdims=True)
            exps[i * n : (i + 1) * n, lanes] = e.astype(bf16)
        out = nn(kv_t[64:256], exps[:, lanes])
        inverse = 1.0 / total
        grad = (g_src[:, cols].astype(f32) * inverse).astype(bf16)
        grads[:, lanes] = grad
        inner = jnp.sum(grad.astype(f32) * out, axis=0, keepdims=True) * inverse
        right = jnp.concatenate([zeros_g, grad], axis=0)
        for i in range(4):
            prob = nn(kv_n[i * n : (i + 1) * n], right)
            e = exps[i * n : (i + 1) * n, lanes].astype(f32)
            score_grads[i * n : (i + 1) * n, lanes] = (e * (prob - inner)).astype(bf16)
        dst[:, cols] = (nn(kv_t[0:64], score_grads[:, lanes]) * SCALE).astype(bf16)
    for i, ref, at in ((2, kv_sib_ref, 0), (3, kv_sib_ref, n), (0, kv_mine_ref, 0), (1, kv_mine_ref, n)):
        key_grad = nt(queries[...], score_grads[i * n : (i + 1) * n]) * SCALE
        ref[0:64, at : at + n] = key_grad.astype(ref.dtype)
        value_grad = nt(grads[...], exps[i * n : (i + 1) * n])
        ref[64:256, at : at + n] = value_grad.astype(ref.dtype)


def join_kernel(q_own, q_par, kv_mine, kv_got, own_ref, par_ref):
    n = q_own.shape[1]
    par_ref[0:64] = q_par[...]
    par_ref[64:320] = (kv_mine[:, n:] + kv_got[:, n:].astype(f32)).astype(bf16)
    own_ref[0:64] = q_own[...]
    own_ref[64:320] = (kv_mine[:, :n] + kv_got[:, :n].astype(f32)).astype(bf16)


def back_kernel(own, other, unit_ref, factor_ref, wq, wk, wv, back, far_ref):
    y = lax.axis_index("tensor")
    chip, _ = own_chip()
    for ref, head in ((own, chip), (other, 1 - chip)):
        for kind in range(2):
            at = pl.ds(pl.multiple_of(kind * 128 + head * KEY, KEY), KEY)
            unit = unit_ref[at]
            factor = factor_ref[pl.ds(kind * 2 + head, 1)]
            g = ref[kind * 64 : kind * 64 + 64].astype(f32)
            mean = jnp.mean(g * unit, axis=0, keepdims=True)
            back[at] = (factor * (g - unit * mean)).astype(bf16)
        back[pl.ds(pl.multiple_of(256 + head * VAL, 64), VAL)] = ref[128:320]
    far_ref[...] = back_rows(back, wq, wk, wv, y ^ 2).astype(bf16)


def back_rows(back, wq, wk, wv, index):
    at = block_at(index, 384)
    qk = jnp.concatenate([wq[at], wk[at]], axis=1)
    return nn(qk, back[0:256]) + nn(wv[at], back[256:640])


def back_near_kernel(back, wq, wk, wv, alone_ref, joined_ref):
    y = lax.axis_index("tensor")
    one, two = distances()
    alone_ref[...] = back_rows(back, wq, wk, wv, y ^ one).astype(bf16)
    joined_ref[...] = back_rows(back, wq, wk, wv, y ^ two)


def back_own_kernel(back, wq, wk, wv, cot, out_ref):
    y = lax.axis_index("tensor")
    out_ref[...] = back_rows(back, wq, wk, wv, y) + cot[...].astype(f32).T


def add_kernel(joined, got, out_ref):
    out_ref[...] = (joined[...] + got[...].astype(f32)).astype(bf16)


def hidden_grad_kernel(own, alone, joined, out_ref):
    out_ref[...] = (own[...] + alone[...].astype(f32) + joined[...].astype(f32)).astype(bf16)


def ring_place():
    x = (lax.axis_index("seq") & 1) * 2 + (lax.axis_index("section") >> 1)
    z = lax.axis_index("seq") >> 1
    return x, z


def tap_own_kernel(taps, grad, out_ref):
    x, _ = ring_place()
    for i, d in enumerate((2, distances()[0])):
        out_ref[i] = nt(taps[block_at(x ^ d, 576)], grad[...])


def tap_add_kernel(index, own, taps, grad, out_ref):
    x, _ = ring_place()
    d = (2, distances()[0])[index]
    out_ref[...] = (own[index] + nt(taps[block_at(x ^ d, 576)], grad[...])).astype(bf16)


def tap_kernel(which, t_mine, t_sib, g_mine, g_sib, out_ref):
    x, _ = ring_place()
    d = (0, *distances(), 2)[which]
    at = block_at(x ^ d, 576)
    out_ref[...] = (nt(t_mine[at], g_mine[...]) + nt(t_sib[at], g_sib[...])).astype(out_ref.dtype)


def sum_x_kernel(own, alone, joined, own_ref, to1, to2, to3):
    _, z = ring_place()
    for d, ref in ((2, to2), (1, to1), (3, to3), (0, own_ref)):
        at = block_at(z ^ d, 144)
        ref[...] = (own[at] + alone[at].astype(f32) + joined[at].astype(f32)).astype(ref.dtype)


def sum_z_kernel(norm, own, r1, r2, r3, out_ref):
    out_ref[...] = (
        own[...] + r1[...].astype(f32) + r2[...].astype(f32) + r3[...].astype(f32)
    ) * norm


def body(bases, stem_w, conv_w, wq, wk, wv, out_w, cot):
    marks = bases[0].T
    cot = cot[0]
    rows = marks.shape[1]
    flat = ("seq", "section")

    low = lax.ppermute(marks, "section", [(i, (i + 1) % 4) for i in range(4)])
    high = lax.ppermute(marks, "section", [((i + 1) % 4, i) for i in range(4)])

    def y_way(value, way):
        pairs = []
        for t in range(4):
            for i in range(4):
                pairs.append((t * 4 + i, (t ^ (1, 3)[(i + way) % 2]) * 4 + i))
        return lax.ppermute(value, ("tensor", "section"), pairs)

    def x_way(value, way):
        return lax.ppermute(value, flat, [(i, i ^ (2 * (1, 3)[(i + way) % 2])) for i in range(32)])

    def over_core(value):
        return lax.ppermute(value, "section", [(i, i ^ 1) for i in range(4)])

    def over_chip(value):
        return lax.ppermute(value, "section", [(i, i ^ 2) for i in range(4)])

    def over_z(value, d):
        return lax.ppermute(value, flat, [(i, i ^ (8 * d)) for i in range(32)])

    second = y_way(cot, 1)
    (act,) = call(stem_kernel, [((rows, 1536), bf16)], marks, stem_w, flops=4e9, vmem=16)
    first = y_way(cot, 0)
    hidden, ext = call(
        conv_kernel,
        [((rows, 384), bf16), ((rows + 2 * HALO, 1536), bf16)],
        marks, low, high, stem_w, act, conv_w,
        flops=2e9,
    )
    cots = [cot, first, second]

    second = y_way(hidden, 1)
    taps_mine, taps_other = call(
        taps_kernel, [((2304, rows), bf16)] * 2, ext,
        scratch=[pltpu.VMEM((1536, rows), bf16)], flops=3e9,
    )
    _, wv_late = lax.optimization_barrier((hidden, wv))
    (w_t,) = call(turn_kernel, [((640, 1536), bf16)], wq, wk, wv_late, flops=1e9)
    tied, cots, taps_mine, w_t = lax.optimization_barrier((hidden, cots, taps_mine, w_t))
    cots = cots + [y_way(cots[2], 0)]
    first = y_way(tied, 0)
    second, cots = lax.optimization_barrier((second, cots))
    far = y_way(second, 0)
    g_own, g_other = call(grad_kernel, [((VAL, rows), bf16)] * 2, *cots, out_w, flops=1e9)
    g_par = over_chip(g_other)
    (part,) = call(project_part_kernel, [((640, rows), f32)], hidden, second, w_t, flops=7e8)
    first, far, part = lax.optimization_barrier((first, far, part))

    own, other, unit, factor = call(
        project_kernel,
        [((320, rows), bf16)] * 2 + [((256, rows), f32), ((4, rows), f32)],
        part, first, far, w_t,
        scratch=[pltpu.VMEM((384, rows), bf16)], flops=1.5e9,
    )
    other, g_par, g_own = lax.optimization_barrier((other, g_par, g_own))
    par = over_chip(other)
    sib_own = over_core(own)
    sib_par = over_core(par)
    taps_sib = over_core(taps_other)
    q_own, q_par, kv_mine, kv_sib = call(
        attend_kernel,
        [((KEY, rows), bf16)] * 2 + [((256, 2 * rows), f32), ((256, 2 * rows), bf16)],
        own, par, sib_own, sib_par, g_own, g_par,
        scratch=[
            pltpu.VMEM((256, 4 * rows), bf16),
            pltpu.VMEM((4 * rows, 256), bf16),
            pltpu.VMEM((4 * rows, 2 * rows), bf16),
            pltpu.VMEM((4 * rows, 2 * rows), bf16),
            pltpu.VMEM((VAL, 2 * rows), bf16),
            pltpu.VMEM((KEY, 2 * rows), bf16),
        ],
        flops=8e9, vmem=48,
    )
    kv_got = over_core(kv_sib)
    back_own, back_par = call(join_kernel, [((320, rows), bf16)] * 2, q_own, q_par, kv_mine, kv_got)
    back_other = over_chip(back_par)
    back, far = call(
        back_kernel,
        [((640, rows), bf16), ((384, rows), bf16)],
        back_own, back_other, unit, factor, wq, wk, wv, flops=5e8,
    )
    got = y_way(far, 0)
    alone, joined = call(
        back_near_kernel, [((384, rows), bf16), ((384, rows), f32)], back, wq, wk, wv, flops=8e8
    )
    alone = y_way(alone, 0)
    (grad_own,) = call(back_own_kernel, [((384, rows), f32)], back, wq, wk, wv, cot, flops=5e8)
    (joined,) = call(add_kernel, [((384, rows), bf16)], joined, got)
    joined = y_way(joined, 1)
    (hg,) = call(hidden_grad_kernel, [((384, rows), bf16)], grad_own, alone, joined)
    hg_sib = over_core(hg)

    def product(which, kind):
        return call(
            functools.partial(tap_kernel, which),
            [((576, 384), kind)],
            taps_mine, taps_sib, hg, hg_sib, flops=6e8,
        )[0]

    (parts,) = call(tap_own_kernel, [((2, 576, 384), f32)], taps_mine, hg, flops=6e8)
    hg_sib, parts = lax.optimization_barrier((hg_sib, parts))
    far, near = [
        call(
            functools.partial(tap_add_kernel, i), [((576, 384), bf16)], parts, taps_sib, hg_sib, flops=3e8
        )[0]
        for i in range(2)
    ]
    got = x_way(far, 0)
    alone = x_way(near, 0)
    joined = product(2, f32)
    part = product(0, f32)
    (joined,) = call(add_kernel, [((576, 384), bf16)], joined, got)
    joined = x_way(joined, 1)
    own_z, z1, z2, z3 = call(
        sum_x_kernel, [((144, 384), f32)] + [((144, 384), bf16)] * 3, part, alone, joined
    )
    got = [over_z(z1, 1), over_z(z3, 3), over_z(z2, 2)]
    norm = 1.0 / math.sqrt(rows * 32)
    (total,) = call(functools.partial(sum_z_kernel, norm), [((144, 384), f32)], own_z, *got)
    return total.reshape(3, 48, 384).transpose(1, 0, 2)


def solution(mesh):
    in_specs = (
        P("seq", "section", None),
        P(),
        P(None, None, "tensor"),
        P(None, "tensor"),
        P(None, "tensor"),
        P(None, "tensor"),
        P("tensor", None),
        P("seq", "section", "tensor"),
    )
    out_specs = P(("seq", "section"), None, "tensor")
    return jax.shard_map(body, mesh=mesh, in_specs=in_specs, out_specs=out_specs, check_vma=False)
```

```python
import functools
import math

import jax
import jax.numpy as jnp
from jax import lax
from jax.experimental import pallas as pl
from jax.experimental.pallas import tpu as pltpu
from jax.sharding import PartitionSpec as P

KEY = 64
VAL = 192
HALO = 32
EPSILON = 1e-06
SCALE = 3.0 / math.sqrt(KEY)
LOG2E = math.log2(math.e)

f32 = jnp.float32
bf16 = jnp.bfloat16
MIB = 1 << 20


def nn(left, right):
    return jnp.dot(left, right, preferred_element_type=f32)


def nt(left, right):
    return lax.dot_general(left, right, (((1,), (1,)), ((), ())), preferred_element_type=f32)


def call(kernel, outs, *args, scratch=(), flops=0, vmem=32, hbm=()):
    size = sum(math.prod(a.shape) * a.dtype.itemsize for a in args)
    return pl.pallas_call(
        kernel,
        out_shape=[jax.ShapeDtypeStruct(shape, kind) for shape, kind in outs],
        in_specs=[
            pl.BlockSpec(memory_space=pl.ANY if i in hbm else pltpu.VMEM) for i in range(len(args))
        ],
        out_specs=[pl.BlockSpec(memory_space=pltpu.VMEM)] * len(outs),
        scratch_shapes=list(scratch),
        compiler_params=pltpu.CompilerParams(vmem_limit_bytes=vmem * MIB),
        cost_estimate=pl.CostEstimate(flops=int(flops), bytes_accessed=int(size), transcendentals=0),
    )(*args)


def own_chip():
    section = lax.axis_index("section")
    return section >> 1, section & 1


def block_at(index, width):
    return pl.ds(pl.multiple_of(index * width, width), width)


def one_hot(marks):
    shape = (128, 32)
    spread = lax.broadcasted_iota(jnp.int32, shape, 0) >> 2 == lax.broadcasted_iota(jnp.int32, shape, 1)
    spread = jnp.where(spread, 1.0, 0.0).astype(bf16)
    wide = nn(spread, marks.astype(f32).astype(bf16))
    letter = (lax.broadcasted_iota(jnp.int32, wide.shape, 0) & 3).astype(f32)
    return jnp.where(wide == letter, 1.0, 0.0).T.astype(bf16)


def gelu(x):
    return jax.nn.gelu(x, approximate=True)


def stem_kernel(marks_ref, stem_ref, act_ref, own_ref):
    hot = one_hot(marks_ref[...])
    own_ref[...] = nn(hot, stem_ref[:, block_at(lax.axis_index("tensor"), 384)])
    for j in range(0, stem_ref.shape[1], 256):
        act_ref[:, j : j + 256] = gelu(nn(hot, stem_ref[:, j : j + 256])).astype(bf16)


def conv_kernel(own_ref, low_ref, high_ref, stem_ref, act_ref, weight_ref, hidden_ref, ext_ref):
    rows = act_ref.shape[0]
    section = lax.axis_index("section")
    edge = one_hot(jnp.concatenate([low_ref[:, rows - HALO :], high_ref[:, :HALO]], axis=1))
    edge_act = gelu(nn(edge, stem_ref[...])).astype(bf16)
    ext_ref[0:HALO] = jnp.where(section > 0, edge_act[:HALO], 0)
    ext_ref[HALO : HALO + rows] = act_ref[...]
    ext_ref[HALO + rows :] = jnp.where(section < 3, edge_act[HALO:], 0)
    total = own_ref[...]
    for k in range(3):
        total = total + nn(ext_ref[k * HALO : k * HALO + rows], weight_ref[k])
    hidden_ref[...] = total.astype(bf16)


def turn_kernel(q_ref, k_ref, v_ref, out_ref):
    out_ref[0:128] = q_ref[...].T
    out_ref[128:256] = k_ref[...].T
    out_ref[256:640] = v_ref[...].T


def taps_kernel(ext_ref, mine_ref, other_ref, turned):
    rows = turned.shape[1]
    _, core = own_chip()
    for k in range(3):
        turned[...] = ext_ref[k * HALO : k * HALO + rows].T
        for x in range(4):
            for z in range(4):
                to = ((x * 4 + z) * 3 + k) * 48
                base = z * 384 + x * 96
                mine_ref[to : to + 48] = turned[pl.ds(pl.multiple_of(base + core * 48, 16), 48)]
                other_ref[to : to + 48] = turned[
                    pl.ds(pl.multiple_of(base + (1 - core) * 48, 16), 48)
                ]


def distances():
    core = lax.axis_index("section") & 1
    return 1 + 2 * core, 3 - 2 * core


def gathered(blocks):
    own, first, second, far = blocks
    one, two = distances()
    return (0, own), (one, first), (two, second), (2, far)


def project_part_kernel(own, second, w_ref, out_ref):
    y = lax.axis_index("tensor")
    _, two = distances()
    out_ref[...] = nt(w_ref[:, block_at(y, 384)], own[...]) + nt(
        w_ref[:, block_at(y ^ two, 384)], second[...]
    )


def project_kernel(part, first, far, w_ref, mine_ref, other_ref, unit_ref, factor_ref, values):
    y = lax.axis_index("tensor")
    chip, _ = own_chip()
    one, _ = distances()
    total = part[...]
    for d, ref in ((one, first), (2, far)):
        total = total + nt(w_ref[:, block_at(y ^ d, 384)], ref[...])
    for g in range(4):
        raw = total[g * KEY : (g + 1) * KEY]
        factor = lax.rsqrt(jnp.mean(raw * raw, axis=0, keepdims=True) + EPSILON)
        unit_ref[g * KEY : (g + 1) * KEY] = raw * factor
        factor_ref[g : g + 1] = factor
    values[...] = total[256:].astype(bf16)
    for ref, head in ((mine_ref, chip), (other_ref, 1 - chip)):
        ref[0:64] = unit_ref[block_at(head, KEY)].astype(bf16)
        ref[64:128] = unit_ref[pl.ds(pl.multiple_of(128 + head * KEY, KEY), KEY)].astype(bf16)
        ref[128:320] = values[block_at(head, VAL)]


def grad_kernel(c0, c1, c2, c3, w_ref, mine_ref, other_ref):
    y = lax.axis_index("tensor")
    chip, _ = own_chip()
    for ref, head in ((mine_ref, chip), (other_ref, 1 - chip)):
        total = 0.0
        for d, block in gathered((c0, c1, c2, c3)):
            total = total + nt(w_ref[block_at(head, VAL), block_at(y ^ d, 384)], block[...])
        ref[...] = total.astype(bf16)


def attend_kernel(
    own, par, sib_own, sib_par, g_own, g_par,
    q_own_ref, q_par_ref, kv_mine_ref, kv_sib_ref,
    kv_t, kv_n, exps, score_grads, grads, queries,
):
    sections = (own, par, sib_own, sib_par)
    n = own.shape[1]
    for i, ref in enumerate(sections):
        kv = ref[64:320]
        kv_t[:, i * n : (i + 1) * n] = kv
        kv_n[i * n : (i + 1) * n] = kv.T
    width = 256
    zeros_q = jnp.zeros((VAL, width), bf16)
    zeros_g = jnp.zeros((KEY, width), bf16)
    for b in range(2 * n // width):
        src, g_src, dst = ((own, g_own, q_own_ref), (par, g_par, q_par_ref))[b * width // n]
        cols = slice((b * width) % n, (b * width) % n + width)
        lanes = slice(b * width, (b + 1) * width)
        query = src[0:64, cols]
        queries[:, lanes] = query
        right = jnp.concatenate([query, zeros_q], axis=0)
        total = jnp.zeros((1, width), f32)
        for i in range(4):
            e = jnp.exp2(nn(kv_n[i * n : (i + 1) * n], right) * (SCALE * LOG2E))
            total = total + jnp.sum(e, axis=0, keepdims=True)
            exps[i * n : (i + 1) * n, lanes] = e.astype(bf16)
        out = nn(kv_t[64:256], exps[:, lanes])
        inverse = 1.0 / total
        grad = (g_src[:, cols].astype(f32) * inverse).astype(bf16)
        grads[:, lanes] = grad
        inner = jnp.sum(grad.astype(f32) * out, axis=0, keepdims=True) * inverse
        right = jnp.concatenate([zeros_g, grad], axis=0)
        for i in range(4):
            prob = nn(kv_n[i * n : (i + 1) * n], right)
            e = exps[i * n : (i + 1) * n, lanes].astype(f32)
            score_grads[i * n : (i + 1) * n, lanes] = (e * (prob - inner)).astype(bf16)
        dst[:, cols] = (nn(kv_t[0:64], score_grads[:, lanes]) * SCALE).astype(bf16)
    for i, ref, at in ((2, kv_sib_ref, 0), (3, kv_sib_ref, n), (0, kv_mine_ref, 0), (1, kv_mine_ref, n)):
        key_grad = nt(queries[...], score_grads[i * n : (i + 1) * n]) * SCALE
        ref[0:64, at : at + n] = key_grad.astype(ref.dtype)
        value_grad = nt(grads[...], exps[i * n : (i + 1) * n])
        ref[64:256, at : at + n] = value_grad.astype(ref.dtype)


def join_kernel(q_own, q_par, kv_mine, kv_got, own_ref, par_ref):
    n = q_own.shape[1]
    par_ref[0:64] = q_par[...]
    par_ref[64:320] = (kv_mine[:, n:] + kv_got[:, n:].astype(f32)).astype(bf16)
    own_ref[0:64] = q_own[...]
    own_ref[64:320] = (kv_mine[:, :n] + kv_got[:, :n].astype(f32)).astype(bf16)


def back_kernel(own, other, unit_ref, factor_ref, wq, wk, wv, back, far_ref):
    y = lax.axis_index("tensor")
    chip, _ = own_chip()
    for ref, head in ((own, chip), (other, 1 - chip)):
        for kind in range(2):
            at = pl.ds(pl.multiple_of(kind * 128 + head * KEY, KEY), KEY)
            unit = unit_ref[at]
            factor = factor_ref[pl.ds(kind * 2 + head, 1)]
            g = ref[kind * 64 : kind * 64 + 64].astype(f32)
            mean = jnp.mean(g * unit, axis=0, keepdims=True)
            back[at] = (factor * (g - unit * mean)).astype(bf16)
        back[pl.ds(pl.multiple_of(256 + head * VAL, 64), VAL)] = ref[128:320]
    far_ref[...] = back_rows(back, wq, wk, wv, y ^ 2).astype(bf16)


def back_rows(back, wq, wk, wv, index):
    at = block_at(index, 384)
    qk = jnp.concatenate([wq[at], wk[at]], axis=1)
    return nn(qk, back[0:256]) + nn(wv[at], back[256:640])


def back_near_kernel(back, wq, wk, wv, alone_ref, joined_ref):
    y = lax.axis_index("tensor")
    one, two = distances()
    alone_ref[...] = back_rows(back, wq, wk, wv, y ^ one).astype(bf16)
    joined_ref[...] = back_rows(back, wq, wk, wv, y ^ two)


def back_own_kernel(back, wq, wk, wv, cot, out_ref):
    y = lax.axis_index("tensor")
    out_ref[...] = back_rows(back, wq, wk, wv, y) + cot[...].astype(f32).T


def add_kernel(joined, got, out_ref):
    out_ref[...] = (joined[...] + got[...].astype(f32)).astype(bf16)


def hidden_grad_kernel(own, alone, joined, out_ref):
    out_ref[...] = (own[...] + alone[...].astype(f32) + joined[...].astype(f32)).astype(bf16)


def ring_place():
    x = (lax.axis_index("seq") & 1) * 2 + (lax.axis_index("section") >> 1)
    z = lax.axis_index("seq") >> 1
    return x, z


def tap_own_kernel(taps, grad, out_ref):
    x, _ = ring_place()
    for i, d in enumerate((2, distances()[0])):
        out_ref[i] = nt(taps[block_at(x ^ d, 576)], grad[...])


def tap_add_kernel(index, own, taps, grad, out_ref):
    x, _ = ring_place()
    d = (2, distances()[0])[index]
    out_ref[...] = (own[index] + nt(taps[block_at(x ^ d, 576)], grad[...])).astype(bf16)


def tap_kernel(which, t_mine, t_sib, g_mine, g_sib, out_ref):
    x, _ = ring_place()
    d = (0, *distances(), 2)[which]
    at = block_at(x ^ d, 576)
    out_ref[...] = (nt(t_mine[at], g_mine[...]) + nt(t_sib[at], g_sib[...])).astype(out_ref.dtype)


def sum_x_kernel(own, alone, joined, own_ref, to1, to2, to3):
    _, z = ring_place()
    for d, ref in ((2, to2), (1, to1), (3, to3), (0, own_ref)):
        at = block_at(z ^ d, 144)
        ref[...] = (own[at] + alone[at].astype(f32) + joined[at].astype(f32)).astype(ref.dtype)


def sum_z_kernel(norm, own, r1, r2, r3, out_ref):
    out_ref[...] = (
        own[...] + r1[...].astype(f32) + r2[...].astype(f32) + r3[...].astype(f32)
    ) * norm


def body(bases, stem_w, conv_w, wq, wk, wv, out_w, cot):
    marks = bases[0].T
    cot = cot[0]
    rows = marks.shape[1]
    flat = ("seq", "section")

    low = lax.ppermute(marks, "section", [(i, (i + 1) % 4) for i in range(4)])
    high = lax.ppermute(marks, "section", [((i + 1) % 4, i) for i in range(4)])

    def y_way(value, way):
        pairs = []
        for t in range(4):
            for i in range(4):
                pairs.append((t * 4 + i, (t ^ (1, 3)[(i + way) % 2]) * 4 + i))
        return lax.ppermute(value, ("tensor", "section"), pairs)

    def x_way(value, way):
        return lax.ppermute(value, flat, [(i, i ^ (2 * (1, 3)[(i + way) % 2])) for i in range(32)])

    def over_core(value):
        return lax.ppermute(value, "section", [(i, i ^ 1) for i in range(4)])

    def over_chip(value):
        return lax.ppermute(value, "section", [(i, i ^ 2) for i in range(4)])

    def over_z(value, d):
        return lax.ppermute(value, flat, [(i, i ^ (8 * d)) for i in range(32)])

    second = y_way(cot, 1)
    act, stem_own = call(stem_kernel, [((rows, 1536), bf16), ((rows, 384), f32)], marks, stem_w, flops=4e9, vmem=16)
    first = y_way(cot, 0)
    hidden, ext = call(
        conv_kernel,
        [((rows, 384), bf16), ((rows + 2 * HALO, 1536), bf16)],
        stem_own, low, high, stem_w, act, conv_w,
        flops=2e9,
    )
    cots = [cot, first, second]

    second = y_way(hidden, 1)
    taps_mine, taps_other = call(
        taps_kernel, [((2304, rows), bf16)] * 2, ext,
        scratch=[pltpu.VMEM((1536, rows), bf16)], flops=3e9,
    )
    _, wv_late = lax.optimization_barrier((hidden, wv))
    (w_t,) = call(turn_kernel, [((640, 1536), bf16)], wq, wk, wv_late, flops=1e9)
    tied, cots, taps_mine, w_t = lax.optimization_barrier((hidden, cots, taps_mine, w_t))
    cots = cots + [y_way(cots[2], 0)]
    first = y_way(tied, 0)
    second, cots = lax.optimization_barrier((second, cots))
    far = y_way(second, 0)
    g_own, g_other = call(grad_kernel, [((VAL, rows), bf16)] * 2, *cots, out_w, flops=1e9)
    g_par = over_chip(g_other)
    (part,) = call(project_part_kernel, [((640, rows), f32)], hidden, second, w_t, flops=7e8)
    first, far, part = lax.optimization_barrier((first, far, part))

    own, other, unit, factor = call(
        project_kernel,
        [((320, rows), bf16)] * 2 + [((256, rows), f32), ((4, rows), f32)],
        part, first, far, w_t,
        scratch=[pltpu.VMEM((384, rows), bf16)], flops=1.5e9,
    )
    other, g_par, g_own = lax.optimization_barrier((other, g_par, g_own))
    par = over_chip(other)
    sib_own = over_core(own)
    sib_par = over_core(par)
    taps_sib = over_core(taps_other)
    q_own, q_par, kv_mine, kv_sib = call(
        attend_kernel,
        [((KEY, rows), bf16)] * 2 + [((256, 2 * rows), f32), ((256, 2 * rows), bf16)],
        own, par, sib_own, sib_par, g_own, g_par,
        scratch=[
            pltpu.VMEM((256, 4 * rows), bf16),
            pltpu.VMEM((4 * rows, 256), bf16),
            pltpu.VMEM((4 * rows, 2 * rows), bf16),
            pltpu.VMEM((4 * rows, 2 * rows), bf16),
            pltpu.VMEM((VAL, 2 * rows), bf16),
            pltpu.VMEM((KEY, 2 * rows), bf16),
        ],
        flops=8e9, vmem=48,
    )
    kv_got = over_core(kv_sib)
    back_own, back_par = call(join_kernel, [((320, rows), bf16)] * 2, q_own, q_par, kv_mine, kv_got)
    back_other = over_chip(back_par)
    back, far = call(
        back_kernel,
        [((640, rows), bf16), ((384, rows), bf16)],
        back_own, back_other, unit, factor, wq, wk, wv, flops=5e8,
    )
    got = y_way(far, 0)
    alone, joined = call(
        back_near_kernel, [((384, rows), bf16), ((384, rows), f32)], back, wq, wk, wv, flops=8e8
    )
    alone = y_way(alone, 0)
    (grad_own,) = call(back_own_kernel, [((384, rows), f32)], back, wq, wk, wv, cot, flops=5e8)
    (joined,) = call(add_kernel, [((384, rows), bf16)], joined, got)
    joined = y_way(joined, 1)
    (hg,) = call(hidden_grad_kernel, [((384, rows), bf16)], grad_own, alone, joined)
    hg_sib = over_core(hg)

    def product(which, kind):
        return call(
            functools.partial(tap_kernel, which),
            [((576, 384), kind)],
            taps_mine, taps_sib, hg, hg_sib, flops=6e8,
        )[0]

    (parts,) = call(tap_own_kernel, [((2, 576, 384), f32)], taps_mine, hg, flops=6e8)
    hg_sib, parts = lax.optimization_barrier((hg_sib, parts))
    far, near = [
        call(
            functools.partial(tap_add_kernel, i), [((576, 384), bf16)], parts, taps_sib, hg_sib, flops=3e8
        )[0]
        for i in range(2)
    ]
    got = x_way(far, 0)
    alone = x_way(near, 0)
    joined = product(2, f32)
    part = product(0, f32)
    (joined,) = call(add_kernel, [((576, 384), bf16)], joined, got)
    joined = x_way(joined, 1)
    own_z, z1, z2, z3 = call(
        sum_x_kernel, [((144, 384), f32)] + [((144, 384), bf16)] * 3, part, alone, joined
    )
    got = [over_z(z1, 1), over_z(z3, 3), over_z(z2, 2)]
    norm = 1.0 / math.sqrt(rows * 32)
    (total,) = call(functools.partial(sum_z_kernel, norm), [((144, 384), f32)], own_z, *got)
    return total.reshape(3, 48, 384).transpose(1, 0, 2)


def solution(mesh):
    in_specs = (
        P("seq", "section", None),
        P(),
        P(None, None, "tensor"),
        P(None, "tensor"),
        P(None, "tensor"),
        P(None, "tensor"),
        P("tensor", None),
        P("seq", "section", "tensor"),
    )
    out_specs = P(("seq", "section"), None, "tensor")
    return jax.shard_map(body, mesh=mesh, in_specs=in_specs, out_specs=out_specs, check_vma=False)
```
